128 devices in a mesh: tp: 8 (over z, y_lo), req: 16 (over y_hi, x, core).
Axes of the slice: x: 4, y: 4 (y_hi: 2, y_lo: 2; y = y_hi * 2 + y_lo), z: 4, core: 2. Of those that a mesh axis runs over, the one named last changes fastest.
Arguments:
- tokens: bfloat16 [8192, 8192], P('req'), may hold values from -6 to 6
- w_query: bfloat16 [8192, 8, 1024], P('req', 'tp'), may hold values from -1 to 1
- w_keyval: bfloat16 [8192, 8, 256], P(None, 'tp'), may hold values from -1 to 1
- output_weight: bfloat16 [8192, 8, 1024], P('req', 'tp'), may hold values from -0.0625 to 0.0625
- cache: bfloat16 [2, 256, 1024, 1024], P(None, 'req', None, 'tp'), may hold values from -6 to 6
- fresh: bfloat16 [2, 4, 256, 1024], P(None, None, 'req', 'tp'), may hold values from -6 to 6
- decode_query: bfloat16 [4, 256, 8192], P(None, 'req', 'tp'), may hold values from -6 to 6
- cache_len: int32 [16, 16], P('req'), may hold values from 1 to 1024, 10240 in all within a row
- new_len: int32 [16, 16], replicated, may hold values from 1 to 64, 512 in all within a row
- route: int32 [16, 16], replicated, may hold values from 0 to 15, each once within a row
Outputs:
- prefill_out: bfloat16 [8192, 8192], P('req', 'tp')
- decode_out: bfloat16 [4, 256, 8192], P(None, 'req', 'tp')
The draws below stay inside these ranges and needn't reach their ends.
Inputs may be any that keep to these rules, and one draw needn't show every extreme that they name: `new_len`: each row sums to 512. `cache_len`: each row of one decode group sums to 10240. `route`: each row is a permutation of 0..15.
All inputs are finite; a program needn't handle non-finite values.
Results may differ from the reference program's by a relative error of at most 0.0065.
Values may be sent and summed in bfloat16 or wider, within the bound.
A program may use at most 128 MiB of HBM per device.

```python
import math
import jax
import jax.numpy as jnp
import numpy as np
from jax import lax

MODEL_WIDTH = 8192
QUERY_HEADS = 64
KEYVALUE_HEADS = 8
HEAD_SIZE = 128
PTOK_DEV = 512
CACHE_ROWS_HELD = 1024
DECODE_STEPS = 4
HEADS_PER_GROUP = 8
REQ_DEV = 16
REQUEST_TOTAL = 256
TOKENS = 8192
NEW_MOST = 64
N_REQ = 16


def draw_tokens(key, part):
    key = jax.random.fold_in(key, 11)
    return jnp.clip(jax.random.normal(key, (TOKENS, MODEL_WIDTH), jnp.float32), -6.0, 6.0).astype(jnp.bfloat16)


def draw_w_query(key, part):
    key = jax.random.fold_in(key, 21)
    return (jnp.clip(jax.random.normal(key, (MODEL_WIDTH, KEYVALUE_HEADS, HEADS_PER_GROUP * HEAD_SIZE), jnp.float32), -6.0, 6.0) / math.sqrt(MODEL_WIDTH)).astype(jnp.bfloat16)


def draw_w_keyval(key, part):
    key = jax.random.fold_in(key, 22)
    return (jnp.clip(jax.random.normal(key, (MODEL_WIDTH, KEYVALUE_HEADS, 2 * HEAD_SIZE), jnp.float32), -6.0, 6.0) / math.sqrt(MODEL_WIDTH)).astype(jnp.bfloat16)


def draw_cache(key, part):
    key = jax.random.fold_in(key, 41)
    array_shape = (2, REQUEST_TOTAL, CACHE_ROWS_HELD, KEYVALUE_HEADS * HEAD_SIZE)
    return jnp.clip(jax.random.normal(key, array_shape, jnp.float32), -6.0, 6.0).astype(jnp.bfloat16)


def draw_fresh(key, part):
    key = jax.random.fold_in(key, 42)
    array_shape = (2, DECODE_STEPS, REQUEST_TOTAL, KEYVALUE_HEADS * HEAD_SIZE)
    return jnp.clip(jax.random.normal(key, array_shape, jnp.float32), -6.0, 6.0).astype(jnp.bfloat16)


def draw_decode_query(key, part):
    key = jax.random.fold_in(key, 43)
    array_shape = (DECODE_STEPS, REQUEST_TOTAL, QUERY_HEADS * HEAD_SIZE)
    return jnp.clip(jax.random.normal(key, array_shape, jnp.float32), -6.0, 6.0).astype(jnp.bfloat16)


def steps_of(own_key, shape, pieces, least, largest):
    def one(dim, blocks):
        draws = jax.random.uniform(jax.random.fold_in(jax.random.fold_in(own_key, 6), dim), (blocks,), jnp.float32, least / len(pieces), largest / len(pieces))
        return jnp.repeat(jnp.exp(draws), shape[dim] // blocks).reshape((-1,) + (1,) * (len(shape) - dim - 1))

    loudness = one(*pieces[0])
    for cut in pieces[1:]:
        loudness = loudness * one(*cut)
    return loudness


def split_up(number_of, total, bound, lean):
    loads = [(1 << 20) // math.isqrt(standing ** lean) + 1 for standing in range(2, number_of + 1)]
    rest, counts = total - bound - (number_of - 1), [1] * (number_of - 1)
    while rest > 0:
        free = [i for i in range(number_of - 1) if counts[i] < bound]
        mass, left = sum([loads[i] for i in free]), rest
        for i in free:
            more = min(bound - counts[i], max(1, left * loads[i] // mass), rest)
            counts[i] = counts[i] + more
            rest = rest - more
    return np.array([bound] + counts)


def ragged(own_key, number_of, total, limit, lean):
    if number_of == 2:
        one = jax.random.randint(own_key, (), max(1, total - limit), min(limit, total - 1) + 1)
        return jnp.stack([one, total - one])
    tallies = jnp.asarray(split_up(number_of, total, limit, lean), jnp.int32)
    couples = (number_of - 1) // 2
    source_of, taker = tallies[1:1 + 2 * couples:2], tallies[2:2 + 2 * couples:2]
    margin = jnp.minimum(source_of - 1, limit - taker)
    shifted = jax.random.randint(jax.random.fold_in(own_key, 1), (couples,), 0, 1 << 20) % (margin + 1)
    tallies = tallies.at[1:1 + 2 * couples:2].set(source_of - shifted).at[2:2 + 2 * couples:2].set(taker + shifted)
    return tallies[jax.random.permutation(jax.random.fold_in(own_key, 2), number_of)]


def scatter_about(key, extent, scale, bound, pieces=(), kind=jnp.bfloat16):
    drawn = jax.random.normal(key, extent, jnp.float32) * scale
    if len(pieces) > 0:
        drawn = steps_of(key, extent, pieces, -0.22, 0.18) * drawn
    return jnp.clip(drawn, min=-bound, max=bound).astype(kind)


def setup_inputs(seed: int = 0) -> dict:
    streams_of = jax.random.split(jax.random.key(seed), 11)
    return {
        "tokens": draw_tokens(jax.random.fold_in(streams_of[10], 71), 0),
        "w_query": draw_w_query(jax.random.fold_in(streams_of[10], 71), 0),
        "w_keyval": draw_w_keyval(jax.random.fold_in(streams_of[10], 71), 0),
        "output_weight": scatter_about(streams_of[3], (MODEL_WIDTH, KEYVALUE_HEADS, HEADS_PER_GROUP * HEAD_SIZE), (QUERY_HEADS * HEAD_SIZE) ** -0.5, 0.0625, ((0, 16), (1, 8))),
        "cache": draw_cache(jax.random.fold_in(streams_of[10], 71), 0),
        "fresh": draw_fresh(jax.random.fold_in(streams_of[10], 71), 0),
        "decode_query": draw_decode_query(jax.random.fold_in(streams_of[10], 71), 0),
        "cache_len": jax.vmap(lambda own: ragged(own, REQ_DEV, REQ_DEV * CACHE_ROWS_HELD * 5 // 8, CACHE_ROWS_HELD, 2))(jax.random.split(streams_of[7], N_REQ)).reshape((N_REQ, REQ_DEV)).astype(jnp.int32),
        "new_len": jax.vmap(lambda own: ragged(own, REQ_DEV, PTOK_DEV, NEW_MOST, 2))(jax.random.split(streams_of[8], N_REQ)).reshape((N_REQ, REQ_DEV)).astype(jnp.int32),
        "route": jax.vmap(lambda own: jax.random.permutation(own, N_REQ))(jax.random.split(streams_of[9], N_REQ)).reshape((N_REQ, REQ_DEV)).astype(jnp.int32),
    }


NEG = -1e30


def segment_ids(lens, count):
    ends = jnp.cumsum(lens).astype(jnp.int32)
    position = jnp.arange(count, dtype=jnp.int32)
    return jnp.sum((position[:, None] >= ends[None, :]).astype(jnp.int32), axis=1)


def prefill_attend(query, keyval, lens):
    count, heads = keyval.shape[0], keyval.shape[1]
    width = keyval.shape[2] // 2
    group = query.shape[2] // width
    scale = width ** -0.5
    seg = segment_ids(lens, count)
    position = jnp.arange(count, dtype=jnp.int32)
    allowed = (seg[:, None] == seg[None, :]) & (position[None, :] <= position[:, None])
    q_four = query.reshape(count, heads, group, width).astype(jnp.float32)
    keys = keyval[:, :, :width].astype(jnp.float32)
    values = keyval[:, :, width:].astype(jnp.float32)
    scores = jnp.einsum("ihgd,jhd->hgij", q_four, keys) * scale
    scores = jnp.where(allowed[None, None], scores, NEG)
    top = jnp.max(scores, axis=-1, keepdims=True)
    expo = jnp.exp(scores - top)
    total = jnp.sum(expo, axis=-1)
    weights = lax.optimization_barrier(expo.astype(jnp.bfloat16)).astype(jnp.float32)
    acc = jnp.einsum("hgij,jhd->ihgd", weights, values)
    mixed = acc / jnp.transpose(total, (2, 0, 1))[..., None]
    return mixed.astype(jnp.bfloat16).reshape(count, heads * group * width)


def decode_attend(query, cache, fresh, stretch, cache_rows, stretch_rows):
    steps, rows = query.shape[0], query.shape[1]
    heads = stretch.shape[2]
    width = stretch.shape[3] // 2
    group = query.shape[2] // (heads * width)
    span = cache.shape[2]
    most = stretch.shape[1]
    scale = width ** -0.5
    f32 = jnp.float32
    q_five = query.reshape(steps, rows, heads, group, width).astype(f32)
    ckeys = cache[0].reshape(rows, span, heads, width).astype(f32)
    cvals = cache[1].reshape(rows, span, heads, width).astype(f32)
    nkeys = stretch[..., :width].astype(f32)
    nvals = stretch[..., width:].astype(f32)
    fkeys = fresh[0].reshape(steps, rows, heads, width).astype(f32)
    fvals = fresh[1].reshape(steps, rows, heads, width).astype(f32)
    s_cache = jnp.einsum("trhgd,rchd->rhtgc", q_five, ckeys) * scale
    s_new = jnp.einsum("trhgd,rnhd->rhtgn", q_five, nkeys) * scale
    s_fresh = jnp.einsum("trhgd,urhd->rhtgu", q_five, fkeys) * scale
    mask_cache = jnp.arange(span, dtype=jnp.int32)[None, :] < cache_rows[:, None]
    mask_new = jnp.arange(most, dtype=jnp.int32)[None, :] < stretch_rows[:, None]
    mask_fresh = jnp.arange(steps)[None, :] <= jnp.arange(steps)[:, None]
    s_cache = jnp.where(mask_cache[:, None, None, None, :], s_cache, NEG)
    s_new = jnp.where(mask_new[:, None, None, None, :], s_new, NEG)
    s_fresh = jnp.where(mask_fresh[None, None, :, None, :], s_fresh, NEG)
    top = jnp.maximum(jnp.maximum(jnp.max(s_cache, axis=-1), jnp.max(s_new, axis=-1)), jnp.max(s_fresh, axis=-1))[..., None]
    e_cache = jnp.exp(s_cache - top)
    e_new = jnp.exp(s_new - top)
    e_fresh = jnp.exp(s_fresh - top)
    total = jnp.sum(e_cache, axis=-1) + jnp.sum(e_new, axis=-1) + jnp.sum(e_fresh, axis=-1)
    w_cache = lax.optimization_barrier(e_cache.astype(jnp.bfloat16)).astype(f32)
    w_new = lax.optimization_barrier(e_new.astype(jnp.bfloat16)).astype(f32)
    w_fresh = lax.optimization_barrier(e_fresh.astype(jnp.bfloat16)).astype(f32)
    acc = jnp.einsum("rhtgc,rchd->trhgd", w_cache, cvals)
    acc = acc + jnp.einsum("rhtgn,rnhd->trhgd", w_new, nvals)
    acc = acc + jnp.einsum("rhtgu,urhd->trhgd", w_fresh, fvals)
    mixed = acc / jnp.transpose(total, (2, 0, 1, 3))[..., None]
    return mixed.astype(jnp.bfloat16).reshape(steps, rows, heads * group * width)


def reference(tokens, w_query, w_keyval, output_weight, cache, fresh, decode_query, cache_len, new_len, route):
    model = tokens.shape[1]
    groups, slots = route.shape[0], route.shape[1]
    count = tokens.shape[0] // groups
    heads = w_keyval.shape[1]
    width = w_keyval.shape[2] // 2
    query = jnp.dot(tokens, w_query.reshape(model, -1), preferred_element_type=jnp.float32).astype(jnp.bfloat16)
    keyval = jnp.dot(tokens, w_keyval.reshape(model, -1), preferred_element_type=jnp.float32).astype(jnp.bfloat16)

    def one_group(index):
        rows_q = lax.dynamic_slice_in_dim(query, index * count, count, 0)
        rows_kv = lax.dynamic_slice_in_dim(keyval, index * count, count, 0)
        return prefill_attend(rows_q.reshape(count, heads, -1), rows_kv.reshape(count, heads, 2 * width), new_len[index])

    mixed = lax.map(one_group, jnp.arange(groups, dtype=jnp.int32)).reshape(groups * count, -1)
    prefill_out = jnp.dot(mixed, output_weight.reshape(model, -1).T, preferred_element_type=jnp.float32).astype(jnp.bfloat16)

    offsets = (jnp.cumsum(new_len, axis=1) - new_len).astype(jnp.int32)
    most = 2 * count // slots
    cols = keyval.shape[1]
    padded = jnp.concatenate([keyval, jnp.zeros((most, cols), jnp.bfloat16)], axis=0)
    steps = decode_query.shape[0]

    def one_decode(dest):
        hit = (route == dest).astype(jnp.int32)
        start = jnp.sum(hit * offsets, axis=1) + jnp.arange(groups, dtype=jnp.int32) * count
        stretch_rows = jnp.sum(hit * new_len, axis=1).astype(jnp.int32)
        index = start[:, None] + jnp.arange(most, dtype=jnp.int32)[None, :]
        stretch = padded[index].reshape(groups, most, heads, 2 * width)
        part_cache = lax.dynamic_slice_in_dim(cache, dest * slots, slots, 1)
        part_fresh = lax.dynamic_slice_in_dim(fresh, dest * slots, slots, 2)
        part_query = lax.dynamic_slice_in_dim(decode_query, dest * slots, slots, 1)
        return decode_attend(part_query, part_cache, part_fresh, stretch, cache_len[dest], stretch_rows)

    outs = lax.map(one_decode, jnp.arange(groups, dtype=jnp.int32))
    decode_out = jnp.transpose(outs, (1, 0, 2, 3)).reshape(steps, groups * slots, -1)
    return prefill_out, decode_out
```

```python
import functools

import jax
import jax.numpy as jnp
from jax import lax
from jax.experimental import pallas as pl
from jax.experimental.pallas import tpu as pltpu
from jax.sharding import PartitionSpec as P

NEG = -1e30
MESH = pl.DeviceIdType.MESH
F32 = jnp.float32
BF16 = jnp.bfloat16

CUT_Q = 256
CUT_O = 384
LAG1 = 1
LAG2 = 2

MOVES = {
    "yA": ((0, 0), "A", (0, 1), "y"),
    "xpA": ((0, 0), "A", (3, 0), "xp"),
    "xmA": ((0, 0), "A", (1, 0), "xm"),
    "xpB": ((0, 0), "B", (3, 0), "xp"),
    "xmB": ((0, 0), "B", (1, 0), "xm"),
    "xpC": ((0, 1), "A", (3, 1), "xp"),
    "xmC": ((0, 1), "A", (1, 1), "xm"),
    "fpA": ((3, 0), "A0", (2, 0), "xp"),
    "fmA": ((1, 0), "A1", (2, 0), "xm"),
    "fpB": ((3, 0), "B0", (2, 0), "xp"),
    "fmB": ((1, 0), "B1", (2, 0), "xm"),
    "fpC": ((3, 1), "A0", (2, 1), "xp"),
    "fmC": ((1, 1), "A1", (2, 1), "xm"),
    "yB0": ((0, 0), "B", (0, 1), "y"),
    "yBm": ((3, 0), "B", (3, 1), "y"),
    "yBp": ((1, 0), "B", (1, 1), "y"),
    "yB2p": ((2, 0), "B0", (2, 1), "y"),
    "yB2m": ((2, 0), "B1", (2, 1), "y"),
}
SLOTS = [(dx, dy) for dy in range(2) for dx in range(4)]
for _slot in SLOTS:
    for _part in "AB":
        MOVES["s%d%d%s" % (_slot + (_part,))] = (_slot, _part, _slot, "sib")
INDEX = {name: i for i, name in enumerate(MOVES)}
N_MOVES = len(MOVES)
FIRST = ["yA", "xpA", "xmA", "s00A", "xpB", "xmB", "yB0", "s00B"]
EVENTS = [
    (["yA"], ["xpC", "xmC", "s01A"], [((0, 1), "A")]),
    (["xpA", "xmA"], ["fpA", "fmA", "s30A", "s10A"], [((3, 0), "A"), ((1, 0), "A")]),
    (["xpB", "xmB"], ["fpB", "fmB", "yBm", "yBp", "s30B", "s10B"], [((3, 0), "B"), ((1, 0), "B")]),
    (["xpC", "xmC"], ["fpC", "fmC", "s31A", "s11A"], [((3, 1), "A"), ((1, 1), "A")]),
    (["fpA", "fmA"], ["s20A"], [((2, 0), "A")]),
    (["fpB", "fmB"], ["yB2p", "yB2m", "s20B"], [((2, 0), "B")]),
    (["yB0"], ["s01B"], [((0, 1), "B")]),
    (["yBm", "yBp"], ["s31B", "s11B"], [((3, 1), "B"), ((1, 1), "B")]),
    (["fpC", "fmC"], ["s21A"], [((2, 1), "A")]),
    (["yB2p", "yB2m"], ["s21B"], [((2, 1), "B")]),
]
UNITS = [((0, 0), "A"), ((0, 0), "B")] + [u for e in EVENTS for u in e[2]]


def where_am_i():
    tp = lax.axis_index("tp")
    req = lax.axis_index("req")
    return tp // 2, tp % 2, req // 8, (req // 2) % 4, req % 2


def neighbours():
    z, ylo, yhi, x, c = where_am_i()
    tp = z * 2 + ylo
    req = yhi * 8 + x * 2 + c
    return {
        "xp": (tp, yhi * 8 + ((x + 1) % 4) * 2 + c),
        "xm": (tp, yhi * 8 + ((x + 3) % 4) * 2 + c),
        "y": (tp, (1 - yhi) * 8 + x * 2 + c),
        "sib": (tp, yhi * 8 + x * 2 + (1 - c)),
        "zp": (((z + 1) % 4) * 2 + ylo, req),
        "zm": (((z + 3) % 4) * 2 + ylo, req),
        "yl": (z * 2 + (1 - ylo), req),
    }


def row_range(part, cut, rows):
    rest = rows - cut
    return {
        "A": (0, cut),
        "A0": (0, cut // 2),
        "A1": (cut // 2, cut // 2),
        "B": (cut, rest),
        "B0": (cut, rest // 2),
        "B1": (cut + rest // 2, rest // 2),
    }[part]


class Gather:
    def __init__(self, buf, cut, send, recv, near):
        self.buf, self.cut, self.send, self.recv, self.near = buf, cut, send, recv, near

    def copy(self, name):
        src, part, dst, way = MOVES[name]
        start, size = row_range(part, self.cut, self.buf.shape[2])
        lane = 1 if way == "sib" else 0
        i = INDEX[name]
        return pltpu.make_async_remote_copy(
            src_ref=self.buf.at[0, src[1] * 4 + src[0], pl.ds(start, size)],
            dst_ref=self.buf.at[lane, dst[1] * 4 + dst[0], pl.ds(start, size)],
            send_sem=self.send.at[i],
            recv_sem=self.recv.at[i],
            device_id=self.near[way],
            device_id_type=MESH,
        )

    def start(self, names):
        for name in names:
            self.copy(name).start()

    def event(self, k):
        waits, starts, _ = EVENTS[k]
        for name in waits:
            self.copy(name).wait_recv()
        self.start(starts)

    def shared(self, unit):
        (dx, dy), part = unit
        self.copy("s%d%d%s" % (dx, dy, part)).wait_recv()

    def finish(self):
        for name in MOVES:
            self.copy(name).wait_send()


def layer_kernel(
    tok_hbm, wq_hbm, wkv_hbm, wo_hbm, bias_ref,
    out_ref, kv_ref,
    tok, wq, wo, acc, query, mixed, rh, rf, ry, wkv,
    qs, qr, os_, or_, hs, hr, fs, fr, ys, yr, tsem, ksem, lsem,
):
    z, ylo, yhi, x, c = where_am_i()
    near = neighbours()
    count = tok.shape[1]
    chunk = tok.shape[2]
    half = count // 2
    scale = 128 ** -0.5

    own_q = pltpu.make_async_copy(wq_hbm, wq.at[0, 0], lsem.at[0])
    own_o = pltpu.make_async_copy(wo_hbm, wo.at[0, 0], lsem.at[1])
    own_q.start()

    barrier = pltpu.get_barrier_semaphore()
    for way in ("xp", "xm", "y", "sib", "zp", "zm", "yl"):
        pl.semaphore_signal(barrier, inc=1, device_id=near[way], device_id_type=MESH)
    pl.semaphore_wait(barrier, 7)

    gq = Gather(wq, CUT_Q, qs, qr, near)
    go = Gather(wo, CUT_O, os_, or_, near)
    own_q.wait()
    gq.start(FIRST)

    def tok_copy(r):
        return pltpu.make_async_copy(tok_hbm.at[:, pl.ds(r * chunk, chunk)], tok.at[r], tsem.at[r])

    def kv_copy(r, slot):
        return pltpu.make_async_copy(wkv_hbm.at[pl.ds(r * chunk, chunk)], wkv.at[slot], ksem.at[slot])

    kv_copy(0, 0).start()
    for r in range(16):
        tok_copy(r).start()
    own_o.start()
    acc[...] = jnp.zeros_like(acc)

    @pl.loop(0, 16)
    def _(r):
        slot = r % 2

        @pl.when(r < 15)
        def _():
            kv_copy(r + 1, 1 - slot).start()

        tok_copy(r).wait()
        kv_copy(r, slot).wait()
        acc[:, 0:256] += jnp.dot(tok[r], wkv[slot], preferred_element_type=F32)

    kv_ref[...] = acc[:, 0:256].astype(BF16)
    acc[...] = jnp.zeros_like(acc)

    def place(unit):
        (dx, dy), part = unit
        return (x + dx) % 4, (yhi + dy) % 2

    def query_unit(unit):
        (dx, dy), part = unit
        slot = dy * 4 + dx
        xs, yhs = place(unit)
        start, size = row_range(part, CUT_Q, chunk)
        gq.shared(unit)

        @pl.loop(0, 8)
        def _(j):
            lane = j // 4
            cols = pl.ds(pl.multiple_of((j % 4) * 256, 256), 256)
            r = yhs * 8 + xs * 2 + c + lane * (1 - 2 * c)
            acc[:, cols] += jnp.dot(
                tok[r, :, start:start + size],
                wq[lane, slot, start:start + size, cols],
                preferred_element_type=F32,
            )

    query_unit(UNITS[0])
    query_unit(UNITS[1])
    waiting = []
    for k in range(len(EVENTS)):
        gq.event(k)
        if k == 4:
            own_o.wait()
            go.start(FIRST)
        for unit in waiting:
            query_unit(unit)
        waiting = EVENTS[k][2]
    for unit in waiting:
        query_unit(unit)
    query[...] = acc[...].astype(BF16)

    for b in range(4):
        first = max(b - 1, 0) * 128
        rows = slice(b * 128, b * 128 + 128)
        q8 = jnp.concatenate([query[rows, h * 128:h * 128 + 128] for h in range(8)], axis=0)
        keys = kv_ref[first:first + 256, 0:128]
        values = kv_ref[first:first + 256, 128:256]
        s = lax.dot_general(q8, keys, (((1,), (1,)), ((), ())), preferred_element_type=F32) * scale
        s = (s.reshape(8, 128, 256) + bias_ref[b][None]).reshape(1024, 256)
        e = jnp.exp(s - jnp.max(s, axis=1, keepdims=True))
        total = jnp.sum(e, axis=1, keepdims=True)
        o = jnp.dot(e.astype(BF16), values, preferred_element_type=F32) / total
        o = o.astype(BF16)
        for h in range(8):
            mixed[rows, h * 128:h * 128 + 128] = o[h * 128:h * 128 + 128]
        if b < 3:
            go.event(b)

    def role(unit):
        xs, yhs = place(unit)
        return (z + 4 - (yhs * 2 + xs // 2)) % 4, xs % 2

    def cols_of(unit):
        start, size = row_range(unit[1], CUT_O, chunk)
        return pl.ds(start, size)

    def slot_of(unit):
        return unit[0][1] * 4 + unit[0][0]

    def half_copy(k, which):
        unit = UNITS[k]
        return pltpu.make_async_remote_copy(
            src_ref=tok.at[pl.ds(2 * slot_of(unit), 2), pl.ds(which * half, half), cols_of(unit)],
            dst_ref=rh.at[slot_of(unit), :, :, cols_of(unit)],
            send_sem=hs.at[k, which],
            recv_sem=hr.at[k, which],
            device_id=near["zm" if which else "zp"],
            device_id_type=MESH,
        )

    def full_copy(k, which):
        unit = UNITS[k]
        return pltpu.make_async_remote_copy(
            src_ref=tok.at[pl.ds(2 * slot_of(unit), 2), :, cols_of(unit)],
            dst_ref=rf.at[role(unit)[1], which, :, :, cols_of(unit)],
            send_sem=fs.at[k],
            recv_sem=fr.at[k, which],
            device_id=near["zm" if which else "zp"],
            device_id_type=MESH,
        )

    def y_copy(k):
        unit = UNITS[k]
        return pltpu.make_async_remote_copy(
            src_ref=tok.at[pl.ds(2 * slot_of(unit), 2), :, cols_of(unit)],
            dst_ref=ry.at[:, :, cols_of(unit)],
            send_sem=ys.at[k],
            recv_sem=yr.at[k],
            device_id=near["yl"],
            device_id_type=MESH,
        )

    def partial_unit(k):
        unit = UNITS[k]
        slot = slot_of(unit)
        start, size = row_range(unit[1], CUT_O, chunk)
        go.shared(unit)

        @pl.loop(0, 2)
        def _(lane):
            tok[2 * slot + lane, :, start:start + size] = lax.dot_general(
                mixed[...],
                wo[lane, slot, start:start + size, :],
                (((1,), (1,)), ((), ())),
                preferred_element_type=F32,
            ).astype(BF16)

        dz, _ = role(unit)

        @pl.when(dz == 2)
        def _():
            half_copy(k, 0).start()
            half_copy(k, 1).start()

    STEP = 64

    def pass_on(k):
        unit = UNITS[k]
        slot = slot_of(unit)
        start, size = row_range(unit[1], CUT_O, chunk)
        dz, _ = role(unit)
        for which in range(2):

            @pl.when(dz == (1 if which else 3))
            def _():
                half_copy(k, which).wait_recv()

                @pl.loop(0, 2 * (half // STEP))
                def _(j):
                    lane = j // (half // STEP)
                    i = pl.multiple_of((j % (half // STEP)) * STEP, STEP)
                    there = tok[2 * slot + lane, pl.ds(i + which * half, STEP), start:start + size]
                    more = rh[slot, lane, pl.ds(i, STEP), start:start + size]
                    tok[2 * slot + lane, pl.ds(i + which * half, STEP), start:start + size] = (
                        there.astype(F32) + more.astype(F32)
                    ).astype(BF16)

                full_copy(k, which).start()

    def collect(k):
        unit = UNITS[k]
        slot = slot_of(unit)
        start, size = row_range(unit[1], CUT_O, chunk)
        dz, ylos = role(unit)

        @pl.when(dz == 0)
        def _():
            full_copy(k, 0).wait_recv()
            full_copy(k, 1).wait_recv()

            def summed(j):
                lane = j // (count // STEP)
                i = pl.multiple_of((j % (count // STEP)) * STEP, STEP)
                rows = pl.ds(i, STEP)
                total = tok[2 * slot + lane, rows, start:start + size].astype(F32)
                total += rf[ylos, 0, lane, rows, start:start + size].astype(F32)
                total += rf[ylos, 1, lane, rows, start:start + size].astype(F32)
                return lane, rows, total

            @pl.when(ylos == ylo)
            def _():
                @pl.loop(0, 2 * (count // STEP))
                def _(j):
                    lane, rows, total = summed(j)
                    acc[rows, pl.ds(pl.multiple_of(lane * chunk + start, 128), size)] = total

            @pl.when(ylos != ylo)
            def _():
                @pl.loop(0, 2 * (count // STEP))
                def _(j):
                    lane, rows, total = summed(j)
                    tok[2 * slot + lane, rows, start:start + size] = total.astype(BF16)

                y_copy(k).start()

    def deliver(k):
        unit = UNITS[k]
        start, size = row_range(unit[1], CUT_O, chunk)
        dz, ylos = role(unit)

        @pl.when((dz == 0) & (ylos == ylo))
        def _():
            y_copy(k).wait_recv()

            @pl.loop(0, 2 * (count // STEP))
            def _(j):
                lane = j // (count // STEP)
                rows = pl.ds(pl.multiple_of((j % (count // STEP)) * STEP, STEP), STEP)
                total = acc[rows, pl.ds(pl.multiple_of(lane * chunk + start, 128), size)]
                total += ry[lane, rows, start:start + size].astype(F32)
                place_ = (c + lane * (1 - 2 * c)) * chunk + start
                out_ref[rows, pl.ds(pl.multiple_of(place_, 128), size)] = total.astype(BF16)

    steps = [(None, [0, 1])]
    at = 2
    for k in range(len(EVENTS)):
        steps.append((k, list(range(at, at + len(EVENTS[k][2])))))
        at += len(EVENTS[k][2])
    done = [0]

    def advance(k):
        partial_unit(k)
        if k >= LAG1:
            pass_on(k - LAG1)
        if k >= LAG2:
            collect(k - LAG2)

    pending = [0, 1] + steps[1][1] + steps[2][1]
    for u in pending:
        advance(u)
    pending = list(steps[3][1])
    for k in range(3, len(EVENTS)):
        go.event(k)
        for u in pending:
            advance(u)
        pending = list(steps[k + 1][1])
    for u in pending:
        advance(u)
    n = len(UNITS)
    for k in range(n - LAG1, n):
        pass_on(k)
    for k in range(n - LAG2, n):
        collect(k)
    for k in range(n):
        deliver(k)

    gq.finish()
    go.finish()
    for k in range(n):
        dz, ylos = role(UNITS[k])

        @pl.when(dz == 2)
        def _():
            half_copy(k, 0).wait_send()
            half_copy(k, 1).wait_send()

        for which in range(2):

            @pl.when(dz == (1 if which else 3))
            def _():
                full_copy(k, which).wait_send()

        @pl.when((dz == 0) & (ylos != ylo))
        def _():
            y_copy(k).wait_send()


def layer(tokens, wq, wkv, wo, bias):
    count, model = tokens.shape
    rows, cols = wq.shape
    any_ = pl.BlockSpec(memory_space=pl.ANY)
    vmem = pl.BlockSpec(memory_space=pltpu.VMEM)
    dma = pltpu.SemaphoreType.DMA
    n = len(UNITS)
    return pl.pallas_call(
        layer_kernel,
        name="layer",
        out_shape=(
            jax.ShapeDtypeStruct((count, cols), BF16),
            jax.ShapeDtypeStruct((count, 256), BF16),
        ),
        in_specs=[any_, any_, any_, any_, vmem],
        out_specs=(vmem, vmem),
        scratch_shapes=[
            pltpu.VMEM((16, count, 512), BF16),
            pltpu.VMEM((2, 8, rows, cols), BF16),
            pltpu.VMEM((2, 8, rows, cols), BF16),
            pltpu.VMEM((count, cols), F32),
            pltpu.VMEM((count, cols), BF16),
            pltpu.VMEM((count, cols), BF16),
            pltpu.VMEM((8, 2, count // 2, 512), BF16),
            pltpu.VMEM((2, 2, 2, count, 512), BF16),
            pltpu.VMEM((2, count, 512), BF16),
            pltpu.VMEM((2, 512, 256), BF16),
            dma((N_MOVES,)), dma((N_MOVES,)), dma((N_MOVES,)), dma((N_MOVES,)),
            dma((n, 2)), dma((n, 2)), dma((n,)), dma((n, 2)), dma((n,)), dma((n,)),
            dma((16,)), dma((2,)), dma((2,)),
        ],
        compiler_params=pltpu.CompilerParams(
            collective_id=0, has_side_effects=True, vmem_limit_bytes=63 * 2**20
        ),
    )(tokens, wq, wkv, wo, bias)


def segment_ids(lens, count):
    ends = jnp.cumsum(lens)
    position = jnp.arange(count, dtype=jnp.int32)
    return jnp.sum((position[:, None] >= ends[None, :]).astype(jnp.int32), axis=1)


def window_bias(lens, count):
    seg = segment_ids(lens, count)
    out = []
    for b in range(count // 128):
        first = max(b - 1, 0) * 128
        rows = jnp.arange(b * 128, b * 128 + 128, dtype=jnp.int32)
        cols = jnp.arange(first, first + 256, dtype=jnp.int32)
        ok = (seg[b * 128:b * 128 + 128, None] == seg[None, first:first + 256]) & (cols[None, :] <= rows[:, None])
        out.append(jnp.where(ok, 0.0, NEG).astype(F32))
    return jnp.stack(out)


def decode_attend(query, cache, fresh, stretch, cache_rows, stretch_rows):
    steps, rows = (query.shape[0], query.shape[1])
    heads = stretch.shape[2]
    width = stretch.shape[3] // 2
    group = query.shape[2] // (heads * width)
    span = cache.shape[2]
    most = stretch.shape[1]
    scale = width ** (-0.5)
    f32 = jnp.float32
    q_five = query.reshape(steps, rows, heads, group, width)
    ckeys = cache[0].reshape(rows, span, heads, width)
    cvals = cache[1].reshape(rows, span, heads, width)
    nkeys = stretch[..., :width]
    nvals = stretch[..., width:]
    fkeys = fresh[0].reshape(steps, rows, heads, width)
    fvals = fresh[1].reshape(steps, rows, heads, width)
    s_cache = jnp.einsum("trhgd,rchd->rhtgc", q_five, ckeys, preferred_element_type=f32) * scale
    s_new = jnp.einsum("trhgd,rnhd->rhtgn", q_five, nkeys, preferred_element_type=f32) * scale
    s_fresh = jnp.einsum("trhgd,urhd->rhtgu", q_five, fkeys, preferred_element_type=f32) * scale
    mask_cache = jnp.arange(span, dtype=jnp.int32)[None, :] < cache_rows[:, None]
    mask_new = jnp.arange(most, dtype=jnp.int32)[None, :] < stretch_rows[:, None]
    mask_fresh = jnp.arange(steps)[None, :] <= jnp.arange(steps)[:, None]
    s_cache = jnp.where(mask_cache[:, None, None, None, :], s_cache, NEG)
    s_new = jnp.where(mask_new[:, None, None, None, :], s_new, NEG)
    s_fresh = jnp.where(mask_fresh[None, None, :, None, :], s_fresh, NEG)
    top = jnp.maximum(
        jnp.maximum(jnp.max(s_cache, axis=-1), jnp.max(s_new, axis=-1)), jnp.max(s_fresh, axis=-1)
    )[..., None]
    e_cache = jnp.exp(s_cache - top)
    e_new = jnp.exp(s_new - top)
    e_fresh = jnp.exp(s_fresh - top)
    total = jnp.sum(e_cache, axis=-1) + jnp.sum(e_new, axis=-1) + jnp.sum(e_fresh, axis=-1)
    acc = jnp.einsum(
        "rhtgc,rchd->trhgd", e_cache.astype(jnp.bfloat16), cvals, preferred_element_type=f32
    )
    acc = acc + jnp.einsum(
        "rhtgn,rnhd->trhgd", e_new.astype(jnp.bfloat16), nvals, preferred_element_type=f32
    )
    acc = acc + jnp.einsum(
        "rhtgu,urhd->trhgd", e_fresh.astype(jnp.bfloat16), fvals, preferred_element_type=f32
    )
    mixed = acc / jnp.transpose(total, (2, 0, 1, 3))[..., None]
    return mixed.astype(jnp.bfloat16).reshape(steps, rows, heads * group * width)


def local(
    tokens, w_query, w_keyval, output_weight, cache, fresh, decode_query, cache_len, new_len, route
):
    count, model = tokens.shape
    heads = w_keyval.shape[1]
    width = w_keyval.shape[2] // 2
    groups, slots = (route.shape[0], route.shape[1])
    my_group = lax.axis_index("req")
    my_lens = lax.dynamic_index_in_dim(new_len, my_group, 0, keepdims=False)
    prefill_out, keyval = layer(
        tokens,
        w_query.reshape(w_query.shape[0], -1),
        w_keyval.reshape(model, -1),
        output_weight.reshape(output_weight.shape[0], -1),
        window_bias(my_lens, count),
    )
    offsets = jnp.cumsum(my_lens) - my_lens
    my_route = lax.dynamic_index_in_dim(route, my_group, 0, keepdims=False)
    ranks = jnp.arange(groups, dtype=jnp.int32)
    hit_send = (my_route[None, :] == ranks[:, None]).astype(jnp.int32)
    start = jnp.sum(hit_send * offsets[None, :], axis=1)
    most = 2 * count // slots
    cols = keyval.shape[1]
    padded = jnp.concatenate([keyval, jnp.zeros((most, cols), jnp.bfloat16)], axis=0)
    index = start[:, None] + jnp.arange(most, dtype=jnp.int32)[None, :]
    outgoing = padded[index]
    incoming = lax.all_to_all(outgoing, "req", split_axis=0, concat_axis=0, tiled=True)
    hit_recv = (route == my_group).astype(jnp.int32)
    stretch_rows = jnp.sum(hit_recv * new_len, axis=1)
    stretch = incoming.reshape(groups, most, heads, 2 * width)
    decode_out = decode_attend(
        decode_query, cache, fresh, stretch, cache_len.reshape(-1), stretch_rows
    )
    return (prefill_out, decode_out)


def solution(mesh):
    placed = (
        P("req", None),
        P("req", "tp", None),
        P(None, "tp", None),
        P("req", "tp", None),
        P(None, "req", None, "tp"),
        P(None, None, "req", "tp"),
        P(None, "req", "tp"),
        P("req", None),
        P(),
        P(),
    )
    return jax.shard_map(
        local,
        mesh=mesh,
        in_specs=placed,
        out_specs=(P("req", "tp"), P(None, "req", "tp")),
        check_vma=False,
    )
```

```python
import functools

import jax
import jax.numpy as jnp
from jax import lax
from jax.experimental import pallas as pl
from jax.experimental.pallas import tpu as pltpu
from jax.sharding import PartitionSpec as P

NEG = -1e30
MESH = pl.DeviceIdType.MESH
F32 = jnp.float32
BF16 = jnp.bfloat16

CUT_Q = 384
START_O = 3

MOVES_A = {
    "yA": ((0, 0), "A", (0, 1), "y"),
    "xpA": ((0, 0), "A", (3, 0), "xp"),
    "xmA": ((0, 0), "A", (1, 0), "xm"),
    "xpC": ((0, 1), "A", (3, 1), "xp"),
    "xmC": ((0, 1), "A", (1, 1), "xm"),
    "fpA": ((3, 0), "A0", (2, 0), "xp"),
    "fmA": ((1, 0), "A1", (2, 0), "xm"),
    "fpC": ((3, 1), "A0", (2, 1), "xp"),
    "fmC": ((1, 1), "A1", (2, 1), "xm"),
}
MOVES_B = {
    "xpB": ((0, 0), "B", (3, 0), "xp"),
    "xmB": ((0, 0), "B", (1, 0), "xm"),
    "fpB": ((3, 0), "B0", (2, 0), "xp"),
    "fmB": ((1, 0), "B1", (2, 0), "xm"),
    "yB0": ((0, 0), "B", (0, 1), "y"),
    "yBm": ((3, 0), "B", (3, 1), "y"),
    "yBp": ((1, 0), "B", (1, 1), "y"),
    "yB2p": ((2, 0), "B0", (2, 1), "y"),
    "yB2m": ((2, 0), "B1", (2, 1), "y"),
}
SLOTS = [(dx, dy) for dy in range(2) for dx in range(4)]


def shares(units):
    return {"s%d%d%s" % (slot + (part,)): (slot, part, slot, "sib") for slot, part in units}


FIRST_Q = ["yA", "xpA", "xmA", "s00A", "xpB", "xmB", "yB0", "s00B"]
EVENTS_Q = [
    (["yA"], ["xpC", "xmC", "s01A"], [((0, 1), "A")]),
    (["xpA", "xmA"], ["fpA", "fmA", "s30A", "s10A"], [((3, 0), "A"), ((1, 0), "A")]),
    (["xpB", "xmB"], ["fpB", "fmB", "yBm", "yBp", "s30B", "s10B"], [((3, 0), "B"), ((1, 0), "B")]),
    (["xpC", "xmC"], ["fpC", "fmC", "s31A", "s11A"], [((3, 1), "A"), ((1, 1), "A")]),
    (["fpA", "fmA"], ["s20A"], [((2, 0), "A")]),
    (["fpB", "fmB"], ["yB2p", "yB2m", "s20B"], [((2, 0), "B")]),
    (["yB0"], ["s01B"], [((0, 1), "B")]),
    (["yBm", "yBp"], ["s31B", "s11B"], [((3, 1), "B"), ((1, 1), "B")]),
    (["fpC", "fmC"], ["s21A"], [((2, 1), "A")]),
    (["yB2p", "yB2m"], ["s21B"], [((2, 1), "B")]),
]
UNITS_Q = [((0, 0), "A"), ((0, 0), "B")] + [u for e in EVENTS_Q for u in e[2]]
MOVES_Q = {**MOVES_A, **MOVES_B, **shares(UNITS_Q)}
FIRST_O = ["xpA", "xmA", "yA", "s00A"]
EVENTS_O = [
    (["yA"], ["xpC", "xmC", "s01A"], [((0, 1), "A")]),
    (["xpA", "xmA"], ["fpA", "fmA", "s30A", "s10A"], [((3, 0), "A"), ((1, 0), "A")]),
    (["xpC", "xmC"], ["fpC", "fmC", "s31A", "s11A"], [((3, 1), "A"), ((1, 1), "A")]),
    (["fpA"], ["s20A0"], [((2, 0), "A0")]),
    (["fmA"], ["s20A1"], [((2, 0), "A1")]),
    (["fpC"], ["s21A0"], [((2, 1), "A0")]),
    (["fmC"], ["s21A1"], [((2, 1), "A1")]),
]
UNITS_O = [((0, 0), "A")] + [u for e in EVENTS_O for u in e[2]]
HALVES = [(u, r, 256) for r in (0, 256) for u in UNITS_O[:4]]
ITEMS = HALVES + [(u, 0, 512) for u in UNITS_O[4:8]] + [(u, r, 256) for u in UNITS_O[8:] for r in (0, 256)]
PLAN = (
    [("mixed", 0), ("part", 0), ("part", 1), ("event", 1), ("part", 2), ("part", 3), ("mixed", 1)]
    + [("part", i) for i in range(4, 8)]
    + [("event", 2), ("collect", 0), ("collect", 1), ("part", 8), ("part", 9)]
    + [("collect", i) for i in range(2, 8)]
    + [("event", 3), ("event", 4), ("part", 10), ("part", 11), ("collect", 8), ("collect", 9)]
    + [("event", 5), ("part", 12), ("part", 13), ("event", 6), ("part", 14), ("part", 15)]
    + [("collect", i) for i in range(10, 16)]
)
MOVES_O = {**MOVES_A, **shares(UNITS_O)}


def where_am_i():
    tp = lax.axis_index("tp")
    req = lax.axis_index("req")
    return tp // 2, tp % 2, req // 8, (req // 2) % 4, req % 2


def neighbours():
    z, ylo, yhi, x, c = where_am_i()
    tp = z * 2 + ylo
    req = yhi * 8 + x * 2 + c
    return {
        "xp": (tp, yhi * 8 + ((x + 1) % 4) * 2 + c),
        "xm": (tp, yhi * 8 + ((x + 3) % 4) * 2 + c),
        "y": (tp, (1 - yhi) * 8 + x * 2 + c),
        "sib": (tp, yhi * 8 + x * 2 + (1 - c)),
        "z1": (((z + 1) % 4) * 2 + ylo, req),
        "z2": (((z + 2) % 4) * 2 + ylo, req),
        "z3": (((z + 3) % 4) * 2 + ylo, req),
        "yl": (z * 2 + (1 - ylo), req),
    }


def row_range(part, cut, rows):
    rest = rows - cut
    return {
        "A": (0, cut),
        "A0": (0, cut // 2),
        "A1": (cut // 2, cut // 2),
        "B": (cut, rest),
        "B0": (cut, rest // 2),
        "B1": (cut + rest // 2, rest // 2),
    }[part]


class Gather:
    def __init__(self, view, moves, events, rows, cut, send, recv, near):
        self.view, self.moves, self.events = view, moves, events
        self.rows, self.cut, self.send, self.recv, self.near = rows, cut, send, recv, near
        self.index = {name: i for i, name in enumerate(moves)}

    def copy(self, name):
        src, part, dst, way = self.moves[name]
        start, size = row_range(part, self.cut, self.rows)
        lane = 1 if way == "sib" else 0
        i = self.index[name]
        return pltpu.make_async_remote_copy(
            src_ref=self.view(0, src[1] * 4 + src[0], pl.ds(start, size)),
            dst_ref=self.view(lane, dst[1] * 4 + dst[0], pl.ds(start, size)),
            send_sem=self.send.at[i],
            recv_sem=self.recv.at[i],
            device_id=self.near[way],
            device_id_type=MESH,
        )

    def start(self, names):
        for name in names:
            self.copy(name).start()

    def event(self, k):
        waits, starts, _ = self.events[k]
        for name in waits:
            self.copy(name).wait_recv()
        self.start(starts)

    def shared(self, unit):
        (dx, dy), part = unit
        self.copy("s%d%d%s" % (dx, dy, part)).wait_recv()

    def finish(self):
        for name in self.moves:
            self.copy(name).wait_send()


def layer_kernel(
    tok_hbm, wq_hbm, wkv_hbm, wo_hbm, bias_ref,
    out_ref, kv_ref,
    tok, wq, wo, acc, query, mixed, rf, wkv,
    qs, qr, os_, or_, ms, mr, ps, pr, fs, fr, ys, yr, tsem, ksem, lsem,
):
    z, ylo, yhi, x, c = where_am_i()
    near = neighbours()
    count = tok.shape[1]
    chunk = tok.shape[2]
    half = chunk // 2
    scale = 128 ** -0.5

    own_q = pltpu.make_async_copy(wq_hbm, wq.at[0, 0], lsem.at[0])
    own_o = pltpu.make_async_copy(
        wo_hbm.at[pl.ds(pl.multiple_of(ylo * half, half), half)], wo.at[0, 0, 0], lsem.at[1]
    )
    own_q.start()

    barrier = pltpu.get_barrier_semaphore()
    for way in near:
        pl.semaphore_signal(barrier, inc=1, device_id=near[way], device_id_type=MESH)
    pl.semaphore_wait(barrier, len(near))

    gq = Gather(lambda lane, slot, rows: wq.at[lane, slot, rows], MOVES_Q, EVENTS_Q, chunk, CUT_Q, qs, qr, near)
    go = Gather(lambda lane, slot, rows: wo.at[lane, slot, :, rows], MOVES_O, EVENTS_O, half, half, os_, or_, near)
    swap_o = pltpu.make_async_remote_copy(
        src_ref=wo_hbm.at[pl.ds(pl.multiple_of((1 - ylo) * half, half), half)],
        dst_ref=wo.at[0, 0, 1],
        send_sem=ps.at[0],
        recv_sem=pr.at[0],
        device_id=near["yl"],
        device_id_type=MESH,
    )
    own_q.wait()
    gq.start(FIRST_Q)

    def tok_copy(r):
        return pltpu.make_async_copy(tok_hbm.at[:, pl.ds(r * chunk, chunk)], tok.at[r], tsem.at[r])

    def kv_copy(r, slot):
        return pltpu.make_async_copy(wkv_hbm.at[pl.ds(r * chunk, chunk)], wkv.at[slot], ksem.at[slot])

    kv_copy(0, 0).start()
    for r in range(16):
        tok_copy(r).start()
    own_o.start()
    acc[...] = jnp.zeros_like(acc)

    @pl.loop(0, 16)
    def _(r):
        slot = r % 2

        @pl.when(r < 15)
        def _():
            kv_copy(r + 1, 1 - slot).start()

        tok_copy(r).wait()
        kv_copy(r, slot).wait()
        acc[:, 0:256] += jnp.dot(tok[r], wkv[slot], preferred_element_type=F32)

    kv_ref[...] = acc[:, 0:256].astype(BF16)
    acc[...] = jnp.zeros_like(acc)

    def place(unit):
        (dx, dy), part = unit
        return (x + dx) % 4, (yhi + dy) % 2

    def slot_of(unit):
        return unit[0][1] * 4 + unit[0][0]

    def query_unit(unit):
        slot = slot_of(unit)
        xs, yhs = place(unit)
        start, size = row_range(unit[1], CUT_Q, chunk)
        gq.shared(unit)

        @pl.loop(0, 8)
        def _(j):
            lane = j // 4
            cols = pl.ds(pl.multiple_of((j % 4) * 256, 256), 256)
            r = yhs * 8 + xs * 2 + c + lane * (1 - 2 * c)
            acc[:, cols] += jnp.dot(
                tok[r, :, start:start + size],
                wq[lane, slot, start:start + size, cols],
                preferred_element_type=F32,
            )

    query_unit(UNITS_Q[0])
    query_unit(UNITS_Q[1])
    waiting = []
    for k in range(len(EVENTS_Q)):
        gq.event(k)
        if k == 1:
            swap_o.start()
        if k == START_O:
            own_o.wait()
            swap_o.wait_recv()
            go.start(FIRST_O)
        for unit in waiting:
            query_unit(unit)
        waiting = EVENTS_Q[k][2]
    for unit in waiting:
        query_unit(unit)
    query[...] = acc[...].astype(BF16)

    def swap_mixed(b):
        rows = pl.ds(b * 256, 256)
        return pltpu.make_async_remote_copy(
            src_ref=mixed.at[0, rows],
            dst_ref=mixed.at[1, rows],
            send_sem=ms.at[b],
            recv_sem=mr.at[b],
            device_id=near["yl"],
            device_id_type=MESH,
        )

    for b in range(4):
        first = max(b - 1, 0) * 128
        rows = slice(b * 128, b * 128 + 128)
        q8 = jnp.concatenate([query[rows, h * 128:h * 128 + 128] for h in range(8)], axis=0)
        keys = kv_ref[first:first + 256, 0:128]
        values = kv_ref[first:first + 256, 128:256]
        s = lax.dot_general(q8, keys, (((1,), (1,)), ((), ())), preferred_element_type=F32) * scale
        s = (s.reshape(8, 128, 256) + bias_ref[b][None]).reshape(1024, 256)
        e = jnp.exp(s - jnp.max(s, axis=1, keepdims=True))
        total = jnp.sum(e, axis=1, keepdims=True)
        o = jnp.dot(e.astype(BF16), values, preferred_element_type=F32) / total
        o = o.astype(BF16)
        for h in range(8):
            mixed[0, rows, h * 128:h * 128 + 128] = o[h * 128:h * 128 + 128]
        if b % 2 == 1:
            swap_mixed(b // 2).start()
        if b == 1:
            go.event(0)

    def role(unit):
        xs, yhs = place(unit)
        zs = yhs * 2 + xs // 2
        return (z + 4 - zs) % 4, zs, xs % 2

    def z_copy(k, dz):
        unit, row, rows = ITEMS[k]
        start, size = row_range(unit[1], half, half)
        return pltpu.make_async_remote_copy(
            src_ref=tok.at[pl.ds(2 * slot_of(unit), 2), pl.ds(row, rows), pl.ds(start, size)],
            dst_ref=rf.at[role(unit)[2], dz - 1, :, pl.ds(row, rows), pl.ds(start, size)],
            send_sem=fs.at[k],
            recv_sem=fr.at[k, dz - 1],
            device_id=near["z%d" % (4 - dz)],
            device_id_type=MESH,
        )

    def out_cols(lane, h, start):
        return pl.multiple_of((c + lane * (1 - 2 * c)) * chunk + h * half + start, 128)

    def y_copy(k, lane):
        unit, row, rows = ITEMS[k]
        start, size = row_range(unit[1], half, half)
        return pltpu.make_async_remote_copy(
            src_ref=tok.at[2 * slot_of(unit) + lane, pl.ds(row, rows), pl.ds(start, size)],
            dst_ref=out_ref.at[pl.ds(row, rows), pl.ds(out_cols(lane, ylo, start), size)],
            send_sem=ys.at[k, lane],
            recv_sem=yr.at[k, lane],
            device_id=near["yl"],
            device_id_type=MESH,
        )

    def part_item(k):
        unit, row, rows = ITEMS[k]
        slot = slot_of(unit)
        start, size = row_range(unit[1], half, half)
        if row == 0:
            go.shared(unit)

        @pl.loop(0, 2)
        def _(lane):
            by_head = (((1,), (1,)), ((), ()))
            total = lax.dot_general(
                mixed[0, row:row + rows],
                wo[lane, slot, 0, start:start + size, :],
                by_head,
                preferred_element_type=F32,
            )
            total += lax.dot_general(
                mixed[1, row:row + rows],
                wo[lane, slot, 1, start:start + size, :],
                by_head,
                preferred_element_type=F32,
            )
            tok[2 * slot + lane, row:row + rows, start:start + size] = total.astype(BF16)

        dz, _, _ = role(unit)
        for d in range(1, 4):

            @pl.when(dz == d)
            def _():
                z_copy(k, d).start()

    STEP = 64

    def collect(k):
        unit, row, rows = ITEMS[k]
        slot = slot_of(unit)
        start, size = row_range(unit[1], half, half)
        dz, _, ylos = role(unit)

        @pl.when(dz == 0)
        def _():
            for d in range(1, 4):
                z_copy(k, d).wait_recv()

            def summed(j):
                lane = j // (rows // STEP)
                at = pl.ds(pl.multiple_of(row + (j % (rows // STEP)) * STEP, STEP), STEP)
                total = tok[2 * slot + lane, at, start:start + size].astype(F32)
                for d in range(3):
                    total += rf[ylos, d, lane, at, start:start + size].astype(F32)
                return lane, at, total.astype(BF16)

            @pl.when(ylos == ylo)
            def _():
                @pl.loop(0, 2 * (rows // STEP))
                def _(j):
                    lane, at, total = summed(j)
                    out_ref[at, pl.ds(out_cols(lane, ylo, start), size)] = total

            @pl.when(ylos != ylo)
            def _():
                @pl.loop(0, 2 * (rows // STEP))
                def _(j):
                    lane, at, total = summed(j)
                    tok[2 * slot + lane, at, start:start + size] = total

                for lane in range(2):
                    y_copy(k, lane).start()

    for what, k in PLAN:
        if what == "mixed":
            swap_mixed(k).wait_recv()
        elif what == "event":
            go.event(k)
        elif what == "part":
            part_item(k)
        else:
            collect(k)

    gq.finish()
    go.finish()
    swap_o.wait_send()
    for b in range(2):
        swap_mixed(b).wait_send()
    for k in range(len(ITEMS)):
        dz, _, ylos = role(ITEMS[k][0])
        for d in range(1, 4):

            @pl.when(dz == d)
            def _():
                z_copy(k, d).wait_send()

        @pl.when((dz == 0) & (ylos != ylo))
        def _():
            for lane in range(2):
                y_copy(k, lane).wait_send()

        @pl.when((dz == 0) & (ylos == ylo))
        def _():
            for lane in range(2):
                y_copy(k, lane).wait_recv()


def layer(tokens, wq, wkv, wo, bias):
    count, model = tokens.shape
    rows, cols = wq.shape
    any_ = pl.BlockSpec(memory_space=pl.ANY)
    vmem = pl.BlockSpec(memory_space=pltpu.VMEM)
    dma = pltpu.SemaphoreType.DMA
    n = len(ITEMS)
    return pl.pallas_call(
        layer_kernel,
        name="layer",
        out_shape=(
            jax.ShapeDtypeStruct((count, cols), BF16),
            jax.ShapeDtypeStruct((count, 256), BF16),
        ),
        in_specs=[any_, any_, any_, any_, vmem],
        out_specs=(vmem, vmem),
        scratch_shapes=[
            pltpu.VMEM((16, count, 512), BF16),
            pltpu.VMEM((2, 8, rows, cols), BF16),
            pltpu.VMEM((2, 8, 2, rows // 2, cols), BF16),
            pltpu.VMEM((count, cols), F32),
            pltpu.VMEM((count, cols), BF16),
            pltpu.VMEM((2, count, cols), BF16),
            pltpu.VMEM((2, 3, 2, count, 256), BF16),
            pltpu.VMEM((2, 512, 256), BF16),
            dma((len(MOVES_Q),)), dma((len(MOVES_Q),)), dma((len(MOVES_O),)), dma((len(MOVES_O),)),
            dma((2,)), dma((2,)), dma((1,)), dma((1,)),
            dma((n,)), dma((n, 3)), dma((n, 2)), dma((n, 2)),
            dma((16,)), dma((2,)), dma((2,)),
        ],
        compiler_params=pltpu.CompilerParams(
            collective_id=0, has_side_effects=True, vmem_limit_bytes=63 * 2**20
        ),
    )(tokens, wq, wkv, wo, bias)


def segment_ids(lens, count):
    ends = jnp.cumsum(lens)
    position = jnp.arange(count, dtype=jnp.int32)
    return jnp.sum((position[:, None] >= ends[None, :]).astype(jnp.int32), axis=1)


def window_bias(lens, count):
    seg = segment_ids(lens, count)
    out = []
    for b in range(count // 128):
        first = max(b - 1, 0) * 128
        rows = jnp.arange(b * 128, b * 128 + 128, dtype=jnp.int32)
        cols = jnp.arange(first, first + 256, dtype=jnp.int32)
        ok = (seg[b * 128:b * 128 + 128, None] == seg[None, first:first + 256]) & (cols[None, :] <= rows[:, None])
        out.append(jnp.where(ok, 0.0, NEG).astype(F32))
    return jnp.stack(out)


def decode_attend(query, cache, fresh, stretch, cache_rows, stretch_rows):
    steps, rows = (query.shape[0], query.shape[1])
    heads = stretch.shape[2]
    width = stretch.shape[3] // 2
    group = query.shape[2] // (heads * width)
    span = cache.shape[2]
    most = stretch.shape[1]
    scale = width ** (-0.5)
    f32 = jnp.float32
    q_five = query.reshape(steps, rows, heads, group, width)
    ckeys = cache[0].reshape(rows, span, heads, width)
    cvals = cache[1].reshape(rows, span, heads, width)
    nkeys = stretch[..., :width]
    nvals = stretch[..., width:]
    fkeys = fresh[0].reshape(steps, rows, heads, width)
    fvals = fresh[1].reshape(steps, rows, heads, width)
    s_cache = jnp.einsum("trhgd,rchd->rhtgc", q_five, ckeys, preferred_element_type=f32) * scale
    s_new = jnp.einsum("trhgd,rnhd->rhtgn", q_five, nkeys, preferred_element_type=f32) * scale
    s_fresh = jnp.einsum("trhgd,urhd->rhtgu", q_five, fkeys, preferred_element_type=f32) * scale
    mask_cache = jnp.arange(span, dtype=jnp.int32)[None, :] < cache_rows[:, None]
    mask_new = jnp.arange(most, dtype=jnp.int32)[None, :] < stretch_rows[:, None]
    mask_fresh = jnp.arange(steps)[None, :] <= jnp.arange(steps)[:, None]
    s_cache = jnp.where(mask_cache[:, None, None, None, :], s_cache, NEG)
    s_new = jnp.where(mask_new[:, None, None, None, :], s_new, NEG)
    s_fresh = jnp.where(mask_fresh[None, None, :, None, :], s_fresh, NEG)
    top = jnp.maximum(
        jnp.maximum(jnp.max(s_cache, axis=-1), jnp.max(s_new, axis=-1)), jnp.max(s_fresh, axis=-1)
    )[..., None]
    e_cache = jnp.exp(s_cache - top)
    e_new = jnp.exp(s_new - top)
    e_fresh = jnp.exp(s_fresh - top)
    total = jnp.sum(e_cache, axis=-1) + jnp.sum(e_new, axis=-1) + jnp.sum(e_fresh, axis=-1)
    acc = jnp.einsum(
        "rhtgc,rchd->trhgd", e_cache.astype(jnp.bfloat16), cvals, preferred_element_type=f32
    )
    acc = acc + jnp.einsum(
        "rhtgn,rnhd->trhgd", e_new.astype(jnp.bfloat16), nvals, preferred_element_type=f32
    )
    acc = acc + jnp.einsum(
        "rhtgu,urhd->trhgd", e_fresh.astype(jnp.bfloat16), fvals, preferred_element_type=f32
    )
    mixed = acc / jnp.transpose(total, (2, 0, 1, 3))[..., None]
    return mixed.astype(jnp.bfloat16).reshape(steps, rows, heads * group * width)


def local(
    tokens, w_query, w_keyval, output_weight, cache, fresh, decode_query, cache_len, new_len, route
):
    count, model = tokens.shape
    heads = w_keyval.shape[1]
    width = w_keyval.shape[2] // 2
    groups, slots = (route.shape[0], route.shape[1])
    my_group = lax.axis_index("req")
    my_lens = lax.dynamic_index_in_dim(new_len, my_group, 0, keepdims=False)
    prefill_out, keyval = layer(
        tokens,
        w_query.reshape(w_query.shape[0], -1),
        w_keyval.reshape(model, -1),
        output_weight.reshape(output_weight.shape[0], -1),
        window_bias(my_lens, count),
    )
    offsets = jnp.cumsum(my_lens) - my_lens
    my_route = lax.dynamic_index_in_dim(route, my_group, 0, keepdims=False)
    ranks = jnp.arange(groups, dtype=jnp.int32)
    hit_send = (my_route[None, :] == ranks[:, None]).astype(jnp.int32)
    start = jnp.sum(hit_send * offsets[None, :], axis=1)
    most = 2 * count // slots
    cols = keyval.shape[1]
    padded = jnp.concatenate([keyval, jnp.zeros((most, cols), jnp.bfloat16)], axis=0)
    index = start[:, None] + jnp.arange(most, dtype=jnp.int32)[None, :]
    outgoing = padded[index]
    incoming = lax.all_to_all(outgoing, "req", split_axis=0, concat_axis=0, tiled=True)
    hit_recv = (route == my_group).astype(jnp.int32)
    stretch_rows = jnp.sum(hit_recv * new_len, axis=1)
    stretch = incoming.reshape(groups, most, heads, 2 * width)
    decode_out = decode_attend(
        decode_query, cache, fresh, stretch, cache_len.reshape(-1), stretch_rows
    )
    return (prefill_out, decode_out)


def solution(mesh):
    placed = (
        P("req", None),
        P("req", "tp", None),
        P(None, "tp", None),
        P("req", "tp", None),
        P(None, "req", None, "tp"),
        P(None, None, "req", "tp"),
        P(None, "req", "tp"),
        P("req", None),
        P(),
        P(),
    )
    return jax.shard_map(
        local,
        mesh=mesh,
        in_specs=placed,
        out_specs=(P("req", "tp"), P(None, "req", "tp")),
        check_vma=False,
    )
```

```python
import functools

import jax
import jax.numpy as jnp
from jax import lax
from jax.experimental import pallas as pl
from jax.experimental.pallas import tpu as pltpu
from jax.sharding import PartitionSpec as P

NEG = -1e30
MESH = pl.DeviceIdType.MESH
F32 = jnp.float32
BF16 = jnp.bfloat16

CUT_Q = 384
START_O = 3

MOVES_A = {
    "yA": ((0, 0), "A", (0, 1), "y"),
    "xpA": ((0, 0), "A", (3, 0), "xp"),
    "xmA": ((0, 0), "A", (1, 0), "xm"),
    "xpC": ((0, 1), "A", (3, 1), "xp"),
    "xmC": ((0, 1), "A", (1, 1), "xm"),
    "fpA": ((3, 0), "A0", (2, 0), "xp"),
    "fmA": ((1, 0), "A1", (2, 0), "xm"),
    "fpC": ((3, 1), "A0", (2, 1), "xp"),
    "fmC": ((1, 1), "A1", (2, 1), "xm"),
}
MOVES_B = {
    "xpB": ((0, 0), "B", (3, 0), "xp"),
    "xmB": ((0, 0), "B", (1, 0), "xm"),
    "fpB": ((3, 0), "B0", (2, 0), "xp"),
    "fmB": ((1, 0), "B1", (2, 0), "xm"),
    "yB0": ((0, 0), "B", (0, 1), "y"),
    "yBm": ((3, 0), "B", (3, 1), "y"),
    "yBp": ((1, 0), "B", (1, 1), "y"),
    "yB2p": ((2, 0), "B0", (2, 1), "y"),
    "yB2m": ((2, 0), "B1", (2, 1), "y"),
}
SLOTS = [(dx, dy) for dy in range(2) for dx in range(4)]


def shares(units):
    return {"s%d%d%s" % (slot + (part,)): (slot, part, slot, "sib") for slot, part in units}


FIRST_Q = ["yA", "xpA", "xmA", "s00A", "xpB", "xmB", "yB0", "s00B"]
EVENTS_Q = [
    (["yA"], ["xpC", "xmC", "s01A"], [((0, 1), "A")]),
    (["xpA", "xmA"], ["fpA", "fmA", "s30A", "s10A"], [((3, 0), "A"), ((1, 0), "A")]),
    (["xpB", "xmB"], ["fpB", "fmB", "yBm", "yBp", "s30B", "s10B"], [((3, 0), "B"), ((1, 0), "B")]),
    (["xpC", "xmC"], ["fpC", "fmC", "s31A", "s11A"], [((3, 1), "A"), ((1, 1), "A")]),
    (["fpA", "fmA"], ["s20A"], [((2, 0), "A")]),
    (["fpB", "fmB"], ["yB2p", "yB2m", "s20B"], [((2, 0), "B")]),
    (["yB0"], ["s01B"], [((0, 1), "B")]),
    (["yBm", "yBp"], ["s31B", "s11B"], [((3, 1), "B"), ((1, 1), "B")]),
    (["fpC", "fmC"], ["s21A"], [((2, 1), "A")]),
    (["yB2p", "yB2m"], ["s21B"], [((2, 1), "B")]),
]
UNITS_Q = [((0, 0), "A"), ((0, 0), "B")] + [u for e in EVENTS_Q for u in e[2]]
MOVES_Q = {**MOVES_A, **MOVES_B, **shares(UNITS_Q)}
FIRST_O = ["xpA", "xmA", "yA", "s00A"]
EVENTS_O = [
    (["yA"], ["xpC", "xmC", "s01A"], [((0, 1), "A")]),
    (["xpA", "xmA"], ["fpA", "fmA", "s30A", "s10A"], [((3, 0), "A"), ((1, 0), "A")]),
    (["xpC", "xmC"], ["fpC", "fmC", "s31A", "s11A"], [((3, 1), "A"), ((1, 1), "A")]),
    (["fpA"], ["s20A0"], [((2, 0), "A0")]),
    (["fmA"], ["s20A1"], [((2, 0), "A1")]),
    (["fpC"], ["s21A0"], [((2, 1), "A0")]),
    (["fmC"], ["s21A1"], [((2, 1), "A1")]),
]
UNITS_O = [((0, 0), "A")] + [u for e in EVENTS_O for u in e[2]]
HALVES = [(u, r, 256) for r in (0, 256) for u in UNITS_O[:4]]
ITEMS = HALVES + [(u, 0, 512) for u in UNITS_O[4:8]] + [(u, r, 256) for u in UNITS_O[8:] for r in (0, 256)]
PLAN = (
    [("mixed", 0), ("part", 0), ("part", 1), ("event", 1), ("part", 2), ("part", 3), ("mixed", 1)]
    + [("part", i) for i in range(4, 8)]
    + [("decode", r) for r in range(9, 13)]
    + [("event", 2), ("collect", 0), ("collect", 1), ("part", 8), ("part", 9)]
    + [("collect", i) for i in range(2, 8)]
    + [("decode", r) for r in range(13, 16)]
    + [("event", 3), ("event", 4), ("part", 10), ("part", 11), ("collect", 8), ("collect", 9)]
    + [("event", 5), ("part", 12), ("part", 13), ("event", 6), ("part", 14), ("part", 15)]
    + [("collect", i) for i in range(10, 16)]
)
MOVES_O = {**MOVES_A, **shares(UNITS_O)}


def where_am_i():
    tp = lax.axis_index("tp")
    req = lax.axis_index("req")
    return tp // 2, tp % 2, req // 8, (req // 2) % 4, req % 2


def neighbours():
    z, ylo, yhi, x, c = where_am_i()
    tp = z * 2 + ylo
    req = yhi * 8 + x * 2 + c
    return {
        "xp": (tp, yhi * 8 + ((x + 1) % 4) * 2 + c),
        "xm": (tp, yhi * 8 + ((x + 3) % 4) * 2 + c),
        "y": (tp, (1 - yhi) * 8 + x * 2 + c),
        "sib": (tp, yhi * 8 + x * 2 + (1 - c)),
        "z1": (((z + 1) % 4) * 2 + ylo, req),
        "z2": (((z + 2) % 4) * 2 + ylo, req),
        "z3": (((z + 3) % 4) * 2 + ylo, req),
        "yl": (z * 2 + (1 - ylo), req),
    }


def row_range(part, cut, rows):
    rest = rows - cut
    return {
        "A": (0, cut),
        "A0": (0, cut // 2),
        "A1": (cut // 2, cut // 2),
        "B": (cut, rest),
        "B0": (cut, rest // 2),
        "B1": (cut + rest // 2, rest // 2),
    }[part]


class Gather:
    def __init__(self, view, moves, events, rows, cut, send, recv, near):
        self.view, self.moves, self.events = view, moves, events
        self.rows, self.cut, self.send, self.recv, self.near = rows, cut, send, recv, near
        self.index = {name: i for i, name in enumerate(moves)}

    def copy(self, name):
        src, part, dst, way = self.moves[name]
        start, size = row_range(part, self.cut, self.rows)
        lane = 1 if way == "sib" else 0
        i = self.index[name]
        return pltpu.make_async_remote_copy(
            src_ref=self.view(0, src[1] * 4 + src[0], pl.ds(start, size)),
            dst_ref=self.view(lane, dst[1] * 4 + dst[0], pl.ds(start, size)),
            send_sem=self.send.at[i],
            recv_sem=self.recv.at[i],
            device_id=self.near[way],
            device_id_type=MESH,
        )

    def start(self, names):
        for name in names:
            self.copy(name).start()

    def event(self, k):
        waits, starts, _ = self.events[k]
        for name in waits:
            self.copy(name).wait_recv()
        self.start(starts)

    def shared(self, unit):
        (dx, dy), part = unit
        self.copy("s%d%d%s" % (dx, dy, part)).wait_recv()

    def finish(self):
        for name in self.moves:
            self.copy(name).wait_send()


def layer_kernel(
    tok_hbm, wq_hbm, wkv_hbm, wo_hbm, bias_ref, cache_hbm, fresh_ref, dq_ref, sel_ref, lens_ref,
    out_ref, dec_ref,
    tok, wq, wo, acc, query, mixed, rf, wkv, kv_ref, outgoing, stretch, cbuf,
    qs, qr, os_, or_, ms, mr, ps, pr, fs, fr, ys, yr, tsem, ksem, lsem, hs, hr, csem,
):
    z, ylo, yhi, x, c = where_am_i()
    near = neighbours()
    count = tok.shape[1]
    chunk = tok.shape[2]
    half = chunk // 2
    scale = 128 ** -0.5

    own_q = pltpu.make_async_copy(wq_hbm, wq.at[0, 0], lsem.at[0])
    own_o = pltpu.make_async_copy(
        wo_hbm.at[pl.ds(pl.multiple_of(ylo * half, half), half)], wo.at[0, 0, 0], lsem.at[1]
    )
    own_q.start()

    tp = z * 2 + ylo
    req = yhi * 8 + x * 2 + c
    groups = stretch.shape[0]
    barrier = pltpu.get_barrier_semaphore()
    for way in ("z1", "z2", "z3", "yl"):
        pl.semaphore_signal(barrier, inc=1, device_id=near[way], device_id_type=MESH)
    for i in range(1, groups):
        pl.semaphore_signal(barrier, inc=1, device_id=(tp, (req + i) % groups), device_id_type=MESH)
    pl.semaphore_wait(barrier, 4 + groups - 1)

    gq = Gather(lambda lane, slot, rows: wq.at[lane, slot, rows], MOVES_Q, EVENTS_Q, chunk, CUT_Q, qs, qr, near)
    go = Gather(lambda lane, slot, rows: wo.at[lane, slot, :, rows], MOVES_O, EVENTS_O, half, half, os_, or_, near)
    swap_o = pltpu.make_async_remote_copy(
        src_ref=wo_hbm.at[pl.ds(pl.multiple_of((1 - ylo) * half, half), half)],
        dst_ref=wo.at[0, 0, 1],
        send_sem=ps.at[0],
        recv_sem=pr.at[0],
        device_id=near["yl"],
        device_id_type=MESH,
    )
    own_q.wait()
    gq.start(FIRST_Q)

    def tok_copy(r):
        return pltpu.make_async_copy(tok_hbm.at[:, pl.ds(r * chunk, chunk)], tok.at[r], tsem.at[r])

    def kv_copy(r, slot):
        return pltpu.make_async_copy(wkv_hbm.at[pl.ds(r * chunk, chunk)], wkv.at[slot], ksem.at[slot])

    kv_copy(0, 0).start()
    for r in range(16):
        tok_copy(r).start()
    own_o.start()
    acc[...] = jnp.zeros_like(acc)

    @pl.loop(0, 16)
    def _(r):
        slot = r % 2

        @pl.when(r < 15)
        def _():
            kv_copy(r + 1, 1 - slot).start()

        tok_copy(r).wait()
        kv_copy(r, slot).wait()
        acc[:, 0:256] += jnp.dot(tok[r], wkv[slot], preferred_element_type=F32)

    kv_ref[...] = acc[:, 0:256].astype(BF16)
    acc[...] = jnp.zeros_like(acc)

    most = stretch.shape[1]
    outgoing[...] = (
        jnp.dot(sel_ref[...], kv_ref[...], preferred_element_type=F32).astype(BF16).reshape(groups, most, 256)
    )

    def handoff(i):
        to = (req + i) % groups
        return pltpu.make_async_remote_copy(
            src_ref=outgoing.at[to],
            dst_ref=stretch.at[req],
            send_sem=hs.at[i],
            recv_sem=hr.at[i],
            device_id=(tp, to),
            device_id_type=MESH,
        )

    for i in range(1, groups):
        handoff(i).start()
    stretch[req] = outgoing[req]

    def cache_copy(r):
        return pltpu.make_async_copy(cache_hbm.at[:, r], cbuf.at[r % 2], csem.at[r % 2])

    cache_copy(0).start()
    cache_copy(1).start()

    def decode(r):
        if r == 0:
            for i in range(1, groups):
                handoff(i).wait_recv()
        cache_copy(r).wait()
        slot = r % 2
        span = cbuf.shape[2]
        by_head = (((1,), (1,)), ((), ()))
        q = dq_ref[r]
        s = lax.dot_general(q, cbuf[slot, 0], by_head, preferred_element_type=F32) * scale
        col = lax.broadcasted_iota(jnp.int32, (32, span), 1)
        s = jnp.where(col < lens_ref[0, r], s, NEG)
        keys = jnp.concatenate([stretch[r, :, 0:128], fresh_ref[r, 0]], axis=0)
        values = jnp.concatenate([stretch[r, :, 128:256], fresh_ref[r, 1]], axis=0)
        t = lax.dot_general(q, keys, by_head, preferred_element_type=F32) * scale
        col = lax.broadcasted_iota(jnp.int32, (32, 2 * most), 1)
        step = lax.broadcasted_iota(jnp.int32, (32, 2 * most), 0) >> 3
        ok = (col < lens_ref[1, r]) | ((col >= most) & (col - most <= step))
        t = jnp.where(ok, t, NEG)
        top = jnp.maximum(jnp.max(s, axis=1, keepdims=True), jnp.max(t, axis=1, keepdims=True))
        e = jnp.exp(s - top)
        f = jnp.exp(t - top)
        total = jnp.sum(e, axis=1, keepdims=True) + jnp.sum(f, axis=1, keepdims=True)
        got = jnp.dot(e.astype(BF16), cbuf[slot, 1], preferred_element_type=F32)
        got += jnp.dot(f.astype(BF16), values, preferred_element_type=F32)
        dec_ref[r] = (got / total).astype(BF16)
        if r + 2 < groups:
            cache_copy(r + 2).start()

    def place(unit):
        (dx, dy), part = unit
        return (x + dx) % 4, (yhi + dy) % 2

    def slot_of(unit):
        return unit[0][1] * 4 + unit[0][0]

    def query_unit(unit):
        slot = slot_of(unit)
        xs, yhs = place(unit)
        start, size = row_range(unit[1], CUT_Q, chunk)
        gq.shared(unit)

        @pl.loop(0, 8)
        def _(j):
            lane = j // 4
            cols = pl.ds(pl.multiple_of((j % 4) * 256, 256), 256)
            r = yhs * 8 + xs * 2 + c + lane * (1 - 2 * c)
            acc[:, cols] += jnp.dot(
                tok[r, :, start:start + size],
                wq[lane, slot, start:start + size, cols],
                preferred_element_type=F32,
            )

    query_unit(UNITS_Q[0])
    query_unit(UNITS_Q[1])
    waiting = []
    for k in range(len(EVENTS_Q)):
        gq.event(k)
        if k == 1:
            swap_o.start()
        if k == START_O:
            own_o.wait()
            swap_o.wait_recv()
            go.start(FIRST_O)
        for unit in waiting:
            query_unit(unit)
        waiting = EVENTS_Q[k][2]
        if k >= 1:
            decode(k - 1)
    for unit in waiting:
        query_unit(unit)
    query[...] = acc[...].astype(BF16)

    def swap_mixed(b):
        rows = pl.ds(b * 256, 256)
        return pltpu.make_async_remote_copy(
            src_ref=mixed.at[0, rows],
            dst_ref=mixed.at[1, rows],
            send_sem=ms.at[b],
            recv_sem=mr.at[b],
            device_id=near["yl"],
            device_id_type=MESH,
        )

    for b in range(4):
        first = max(b - 1, 0) * 128
        rows = slice(b * 128, b * 128 + 128)
        q8 = jnp.concatenate([query[rows, h * 128:h * 128 + 128] for h in range(8)], axis=0)
        keys = kv_ref[first:first + 256, 0:128]
        values = kv_ref[first:first + 256, 128:256]
        s = lax.dot_general(q8, keys, (((1,), (1,)), ((), ())), preferred_element_type=F32) * scale
        s = (s.reshape(8, 128, 256) + bias_ref[b][None]).reshape(1024, 256)
        e = jnp.exp(s - jnp.max(s, axis=1, keepdims=True))
        total = jnp.sum(e, axis=1, keepdims=True)
        o = jnp.dot(e.astype(BF16), values, preferred_element_type=F32) / total
        o = o.astype(BF16)
        for h in range(8):
            mixed[0, rows, h * 128:h * 128 + 128] = o[h * 128:h * 128 + 128]
        if b % 2 == 1:
            swap_mixed(b // 2).start()
        if b == 1:
            go.event(0)

    def role(unit):
        xs, yhs = place(unit)
        zs = yhs * 2 + xs // 2
        return (z + 4 - zs) % 4, zs, xs % 2

    def z_copy(k, dz):
        unit, row, rows = ITEMS[k]
        start, size = row_range(unit[1], half, half)
        return pltpu.make_async_remote_copy(
            src_ref=tok.at[pl.ds(2 * slot_of(unit), 2), pl.ds(row, rows), pl.ds(start, size)],
            dst_ref=rf.at[role(unit)[2], dz - 1, :, pl.ds(row, rows), pl.ds(start, size)],
            send_sem=fs.at[k],
            recv_sem=fr.at[k, dz - 1],
            device_id=near["z%d" % (4 - dz)],
            device_id_type=MESH,
        )

    def out_cols(lane, h, start):
        return pl.multiple_of((c + lane * (1 - 2 * c)) * chunk + h * half + start, 128)

    def y_copy(k, lane):
        unit, row, rows = ITEMS[k]
        start, size = row_range(unit[1], half, half)
        return pltpu.make_async_remote_copy(
            src_ref=tok.at[2 * slot_of(unit) + lane, pl.ds(row, rows), pl.ds(start, size)],
            dst_ref=out_ref.at[pl.ds(row, rows), pl.ds(out_cols(lane, ylo, start), size)],
            send_sem=ys.at[k, lane],
            recv_sem=yr.at[k, lane],
            device_id=near["yl"],
            device_id_type=MESH,
        )

    def part_item(k):
        unit, row, rows = ITEMS[k]
        slot = slot_of(unit)
        start, size = row_range(unit[1], half, half)
        if row == 0:
            go.shared(unit)

        @pl.loop(0, 2)
        def _(lane):
            by_head = (((1,), (1,)), ((), ()))
            total = lax.dot_general(
                mixed[0, row:row + rows],
                wo[lane, slot, 0, start:start + size, :],
                by_head,
                preferred_element_type=F32,
            )
            total += lax.dot_general(
                mixed[1, row:row + rows],
                wo[lane, slot, 1, start:start + size, :],
                by_head,
                preferred_element_type=F32,
            )
            tok[2 * slot + lane, row:row + rows, start:start + size] = total.astype(BF16)

        dz, _, _ = role(unit)
        for d in range(1, 4):

            @pl.when(dz == d)
            def _():
                z_copy(k, d).start()

    STEP = 64

    def collect(k):
        unit, row, rows = ITEMS[k]
        slot = slot_of(unit)
        start, size = row_range(unit[1], half, half)
        dz, _, ylos = role(unit)

        @pl.when(dz == 0)
        def _():
            for d in range(1, 4):
                z_copy(k, d).wait_recv()

            def summed(j):
                lane = j // (rows // STEP)
                at = pl.ds(pl.multiple_of(row + (j % (rows // STEP)) * STEP, STEP), STEP)
                total = tok[2 * slot + lane, at, start:start + size].astype(F32)
                for d in range(3):
                    total += rf[ylos, d, lane, at, start:start + size].astype(F32)
                return lane, at, total.astype(BF16)

            @pl.when(ylos == ylo)
            def _():
                @pl.loop(0, 2 * (rows // STEP))
                def _(j):
                    lane, at, total = summed(j)
                    out_ref[at, pl.ds(out_cols(lane, ylo, start), size)] = total

            @pl.when(ylos != ylo)
            def _():
                @pl.loop(0, 2 * (rows // STEP))
                def _(j):
                    lane, at, total = summed(j)
                    tok[2 * slot + lane, at, start:start + size] = total

                for lane in range(2):
                    y_copy(k, lane).start()

    for what, k in PLAN:
        if what == "mixed":
            swap_mixed(k).wait_recv()
        elif what == "event":
            go.event(k)
        elif what == "part":
            part_item(k)
        elif what == "decode":
            decode(k)
        else:
            collect(k)

    gq.finish()
    go.finish()
    swap_o.wait_send()
    for i in range(1, groups):
        handoff(i).wait_send()
    for b in range(2):
        swap_mixed(b).wait_send()
    for k in range(len(ITEMS)):
        dz, _, ylos = role(ITEMS[k][0])
        for d in range(1, 4):

            @pl.when(dz == d)
            def _():
                z_copy(k, d).wait_send()

        @pl.when((dz == 0) & (ylos != ylo))
        def _():
            for lane in range(2):
                y_copy(k, lane).wait_send()

        @pl.when((dz == 0) & (ylos == ylo))
        def _():
            for lane in range(2):
                y_copy(k, lane).wait_recv()


def layer(tokens, wq, wkv, wo, bias, cache, fresh, decode_query, sel, lens):
    count, model = tokens.shape
    requests, most, span = (fresh.shape[0], fresh.shape[2], cache.shape[2])
    rows, cols = wq.shape
    any_ = pl.BlockSpec(memory_space=pl.ANY)
    vmem = pl.BlockSpec(memory_space=pltpu.VMEM)
    dma = pltpu.SemaphoreType.DMA
    n = len(ITEMS)
    return pl.pallas_call(
        layer_kernel,
        name="layer",
        out_shape=(
            jax.ShapeDtypeStruct((count, cols), BF16),
            jax.ShapeDtypeStruct(decode_query.shape, BF16),
        ),
        in_specs=[any_, any_, any_, any_, vmem, any_, vmem, vmem, vmem, pl.BlockSpec(memory_space=pltpu.SMEM)],
        out_specs=(vmem, vmem),
        scratch_shapes=[
            pltpu.VMEM((16, count, 512), BF16),
            pltpu.VMEM((2, 8, rows, cols), BF16),
            pltpu.VMEM((2, 8, 2, rows // 2, cols), BF16),
            pltpu.VMEM((count, cols), F32),
            pltpu.VMEM((count, cols), BF16),
            pltpu.VMEM((2, count, cols), BF16),
            pltpu.VMEM((2, 3, 2, count, 256), BF16),
            pltpu.VMEM((2, 512, 256), BF16),
            pltpu.VMEM((count, 256), BF16),
            pltpu.VMEM((requests, most, 256), BF16),
            pltpu.VMEM((requests, most, 256), BF16),
            pltpu.VMEM((2, 2, span, 128), BF16),
            dma((len(MOVES_Q),)), dma((len(MOVES_Q),)), dma((len(MOVES_O),)), dma((len(MOVES_O),)),
            dma((2,)), dma((2,)), dma((1,)), dma((1,)),
            dma((n,)), dma((n, 3)), dma((n, 2)), dma((n, 2)),
            dma((16,)), dma((2,)), dma((2,)), dma((requests,)), dma((requests,)), dma((2,)),
        ],
        compiler_params=pltpu.CompilerParams(
            collective_id=0, has_side_effects=True, vmem_limit_bytes=63 * 2**20
        ),
    )(tokens, wq, wkv, wo, bias, cache, fresh, decode_query, sel, lens)


def segment_ids(lens, count):
    ends = jnp.cumsum(lens)
    position = jnp.arange(count, dtype=jnp.int32)
    return jnp.sum((position[:, None] >= ends[None, :]).astype(jnp.int32), axis=1)


def window_bias(lens, count):
    seg = segment_ids(lens, count)
    out = []
    for b in range(count // 128):
        first = max(b - 1, 0) * 128
        rows = jnp.arange(b * 128, b * 128 + 128, dtype=jnp.int32)
        cols = jnp.arange(first, first + 256, dtype=jnp.int32)
        ok = (seg[b * 128:b * 128 + 128, None] == seg[None, first:first + 256]) & (cols[None, :] <= rows[:, None])
        out.append(jnp.where(ok, 0.0, NEG).astype(F32))
    return jnp.stack(out)


def local(
    tokens, w_query, w_keyval, output_weight, cache, fresh, decode_query, cache_len, new_len, route
):
    count, model = tokens.shape
    groups, slots = (route.shape[0], route.shape[1])
    steps, rows, qcols = decode_query.shape
    width = w_keyval.shape[2] // 2
    heads = qcols // width
    most = 2 * count // slots
    my_group = lax.axis_index("req")
    my_lens = lax.dynamic_index_in_dim(new_len, my_group, 0, keepdims=False)
    offsets = jnp.cumsum(my_lens) - my_lens
    my_route = lax.dynamic_index_in_dim(route, my_group, 0, keepdims=False)
    ranks = jnp.arange(groups, dtype=jnp.int32)
    hit_send = (my_route[None, :] == ranks[:, None]).astype(jnp.int32)
    start = jnp.sum(hit_send * offsets[None, :], axis=1)
    index = (start[:, None] + jnp.arange(most, dtype=jnp.int32)[None, :]).reshape(-1)
    sel = (index[:, None] == jnp.arange(count, dtype=jnp.int32)[None, :]).astype(jnp.bfloat16)
    hit_recv = (route == my_group).astype(jnp.int32)
    stretch_rows = jnp.sum(hit_recv * new_len, axis=1)
    lens = jnp.stack([cache_len.reshape(-1), stretch_rows])
    extra = jnp.pad(jnp.transpose(fresh, (2, 0, 1, 3)), ((0, 0), (0, 0), (0, most - steps), (0, 0)))
    dq = decode_query.reshape(steps, rows, heads, width).transpose(1, 0, 2, 3).reshape(rows, steps * heads, width)
    prefill_out, decoded = layer(
        tokens,
        w_query.reshape(w_query.shape[0], -1),
        w_keyval.reshape(model, -1),
        output_weight.reshape(output_weight.shape[0], -1),
        window_bias(my_lens, count),
        cache,
        extra,
        dq,
        sel,
        lens,
    )
    decode_out = decoded.reshape(rows, steps, heads, width).transpose(1, 0, 2, 3).reshape(steps, rows, qcols)
    return (prefill_out, decode_out)


def solution(mesh):
    placed = (
        P("req", None),
        P("req", "tp", None),
        P(None, "tp", None),
        P("req", "tp", None),
        P(None, "req", None, "tp"),
        P(None, None, "req", "tp"),
        P(None, "req", "tp"),
        P("req", None),
        P(),
        P(),
    )
    return jax.shard_map(
        local,
        mesh=mesh,
        in_specs=placed,
        out_specs=(P("req", "tp"), P(None, "req", "tp")),
        check_vma=False,
    )
```

```python
import functools

import jax
import jax.numpy as jnp
from jax import lax
from jax.experimental import pallas as pl
from jax.experimental.pallas import tpu as pltpu
from jax.sharding import PartitionSpec as P

NEG = -1e30
MESH = pl.DeviceIdType.MESH
F32 = jnp.float32
BF16 = jnp.bfloat16

CUT_Q = 384
CUT_O = 128
START_O = 3

MOVES = {
    "yA": ((0, 0), "A", (0, 1), "y"),
    "xpA": ((0, 0), "A", (3, 0), "xp"),
    "xmA": ((0, 0), "A", (1, 0), "xm"),
    "xpB": ((0, 0), "B", (3, 0), "xp"),
    "xmB": ((0, 0), "B", (1, 0), "xm"),
    "xpC": ((0, 1), "A", (3, 1), "xp"),
    "xmC": ((0, 1), "A", (1, 1), "xm"),
    "fpA": ((3, 0), "A0", (2, 0), "xp"),
    "fmA": ((1, 0), "A1", (2, 0), "xm"),
    "fpC": ((3, 1), "A0", (2, 1), "xp"),
    "fmC": ((1, 1), "A1", (2, 1), "xm"),
    "fpB": ((3, 0), "B0", (2, 0), "xp"),
    "fmB": ((1, 0), "B1", (2, 0), "xm"),
    "yB0": ((0, 0), "B", (0, 1), "y"),
    "yBm": ((3, 0), "B", (3, 1), "y"),
    "yBp": ((1, 0), "B", (1, 1), "y"),
    "yB2p": ((2, 0), "B0", (2, 1), "y"),
    "yB2m": ((2, 0), "B1", (2, 1), "y"),
}
FIRST_A = ["yA", "xpA", "xmA", "s00A"]
FIRST_B = ["xpB", "xmB", "yB0", "s00B"]
EVENTS = [
    (["yA"], ["xpC", "xmC", "s01A"], [((0, 1), "A")]),
    (["xpA", "xmA"], ["fpA", "fmA", "s30A", "s10A"], [((3, 0), "A"), ((1, 0), "A")]),
    (["xpB", "xmB"], ["fpB", "fmB", "yBm", "yBp", "s30B", "s10B"], [((3, 0), "B"), ((1, 0), "B")]),
    (["xpC", "xmC"], ["fpC", "fmC", "s31A", "s11A"], [((3, 1), "A"), ((1, 1), "A")]),
    (["fpA", "fmA"], ["s20A"], [((2, 0), "A")]),
    (["fpB", "fmB"], ["yB2p", "yB2m", "s20B"], [((2, 0), "B")]),
    (["yB0"], ["s01B"], [((0, 1), "B")]),
    (["yBm", "yBp"], ["s31B", "s11B"], [((3, 1), "B"), ((1, 1), "B")]),
    (["fpC", "fmC"], ["s21A"], [((2, 1), "A")]),
    (["yB2p", "yB2m"], ["s21B"], [((2, 1), "B")]),
]
UNITS = [((0, 0), "A"), ((0, 0), "B")] + [u for e in EVENTS for u in e[2]]
MOVES_ALL = {**MOVES, **{"s%d%d%s" % (slot + (part,)): (slot, part, slot, "sib") for slot, part in UNITS}}
EVENTS_O = [EVENTS[k] for k in (2, 0, 1, 5, 3, 4, 6, 7, 8, 9)]
START_1 = ["xpB", "xmB", "yA", "s00B"]
START_2 = ["xpA", "xmA", "yB0", "s00A"]
EARLY = [((0, 0), "AB"), ((0, 1), "A"), ((3, 0), "AB"), ((1, 0), "AB")]
LATE = [((3, 1), "A"), ((1, 1), "A"), ((2, 0), "AB"), ((0, 1), "B"), ((3, 1), "B"), ((1, 1), "B"), ((2, 1), "A"), ((2, 1), "B")]
ITEMS = [e + (r, 256) for r in (0, 256) for e in EARLY] + [e + (0, 512) for e in LATE]


def span(what, first, last):
    return [(what, k) for k in range(first, last)]


PLAN = (
    [("event", 2), ("mixed", 0)] + span("part", 0, 2) + [("event", 3)] + span("part", 2, 4) + [("mixed", 1)] + span("part", 4, 8)
    + [("event", 4)] + span("decode", 9, 13) + span("part", 8, 10) + [("event", 5), ("part", 10), ("event", 6), ("part", 11)]
    + span("decode", 13, 16) + span("collect", 0, 4) + [("event", 7)] + span("part", 12, 14) + span("collect", 4, 8)
    + [("event", 8), ("part", 14), ("event", 9), ("part", 15)] + span("collect", 8, 16)
)


def where_am_i():
    tp = lax.axis_index("tp")
    req = lax.axis_index("req")
    return tp // 2, tp % 2, req // 8, (req // 2) % 4, req % 2


def neighbours():
    z, ylo, yhi, x, c = where_am_i()
    tp = z * 2 + ylo
    req = yhi * 8 + x * 2 + c
    return {
        "xp": (tp, yhi * 8 + ((x + 1) % 4) * 2 + c),
        "xm": (tp, yhi * 8 + ((x + 3) % 4) * 2 + c),
        "y": (tp, (1 - yhi) * 8 + x * 2 + c),
        "y3": (z * 2 + (1 - ylo), (1 - yhi) * 8 + x * 2 + c),
        "sib": (tp, yhi * 8 + x * 2 + (1 - c)),
        "z1": (((z + 1) % 4) * 2 + ylo, req),
        "z2": (((z + 2) % 4) * 2 + ylo, req),
        "z3": (((z + 3) % 4) * 2 + ylo, req),
        "yl": (z * 2 + (1 - ylo), req),
    }


def row_range(part, cut, rows):
    rest = rows - cut
    return {
        "A": (0, cut),
        "A0": (0, cut // 2),
        "A1": (cut // 2, cut // 2),
        "B": (cut, rest),
        "B0": (cut, rest // 2),
        "B1": (cut + rest // 2, rest // 2),
        "AB": (0, rows),
    }[part]


class Gather:
    def __init__(self, view, events, rows, cut, send, recv, near):
        self.view, self.moves, self.events = view, MOVES_ALL, events
        self.rows, self.cut, self.send, self.recv, self.near = rows, cut, send, recv, near
        self.index = {name: i for i, name in enumerate(MOVES_ALL)}

    def copy(self, name):
        src, part, dst, way = self.moves[name]
        start, size = row_range(part, self.cut, self.rows)
        lane = 1 if way == "sib" else 0
        i = self.index[name]
        return pltpu.make_async_remote_copy(
            src_ref=self.view(0, src[1] * 4 + src[0], pl.ds(start, size)),
            dst_ref=self.view(lane, dst[1] * 4 + dst[0], pl.ds(start, size)),
            send_sem=self.send.at[i],
            recv_sem=self.recv.at[i],
            device_id=self.near[way],
            device_id_type=MESH,
        )

    def start(self, names):
        for name in names:
            self.copy(name).start()

    def event(self, k):
        waits, starts, _ = self.events[k]
        for name in waits:
            self.copy(name).wait_recv()
        self.start(starts)

    def shared(self, slot, parts):
        for part in parts:
            self.copy("s%d%d%s" % (slot + (part,))).wait_recv()

    def finish(self):
        for name in self.moves:
            self.copy(name).wait_send()


def layer_kernel(
    tok_hbm, wq_hbm, wkv_hbm, wo_hbm, cache_hbm, fresh_ref, dq_ref, held_ref, new_ref, route_ref,
    out_ref, dec_ref,
    tok, wq, wo, acc, query, mixed, rf, wkv, kvs, outgoing, stretch, cbuf,
    qs, qr, os_, or_, ms, mr, ps, pr, fs, fr, ys, yr, tsem, ksem, lsem, hs, hr, csem,
):
    z, ylo, yhi, x, c = where_am_i()
    near = neighbours()
    count = tok.shape[1]
    chunk = tok.shape[2]
    half = chunk // 2
    scale = 128 ** -0.5

    e = (ylo + yhi) % 2
    own_half = pl.ds(pl.multiple_of(e * half, half), half)
    other_half = pl.ds(pl.multiple_of((1 - e) * half, half), half)
    own_q = pltpu.make_async_copy(wq_hbm, wq.at[0, 0], lsem.at[0])
    own_o = pltpu.make_async_copy(wo_hbm.at[own_half], wo.at[0, 0, ylo], lsem.at[1])
    own_q.start()
    own_o.start()

    tp = z * 2 + ylo
    req = yhi * 8 + x * 2 + c
    groups = stretch.shape[0]
    barrier = pltpu.get_barrier_semaphore()
    for way in ("z1", "z2", "z3", "yl", "y3"):
        pl.semaphore_signal(barrier, inc=1, device_id=near[way], device_id_type=MESH)
    for i in range(1, groups):
        pl.semaphore_signal(barrier, inc=1, device_id=(tp, (req + i) % groups), device_id_type=MESH)
    pl.semaphore_wait(barrier, 5 + groups - 1)

    gq = Gather(lambda lane, slot, rows: wq.at[lane, slot, rows], EVENTS, chunk, CUT_Q, qs, qr, near)
    go = Gather(
        lambda lane, slot, rows: wo.at[lane, slot, :, rows], EVENTS_O, half, CUT_O, os_, or_, {**near, "y": near["y3"]}
    )
    swap_o = pltpu.make_async_remote_copy(
        src_ref=wo_hbm.at[other_half],
        dst_ref=wo.at[0, 0, ylo],
        send_sem=ps.at[0],
        recv_sem=pr.at[0],
        device_id=near["yl"],
        device_id_type=MESH,
    )
    own_q.wait()
    gq.start(FIRST_A)
    gq.start(FIRST_B)

    def tok_copy(r):
        return pltpu.make_async_copy(tok_hbm.at[:, pl.ds(r * chunk, chunk)], tok.at[r], tsem.at[r])

    def kv_copy(r, slot):
        return pltpu.make_async_copy(wkv_hbm.at[pl.ds(r * chunk, chunk)], wkv.at[slot], ksem.at[slot])

    kv_copy(0, 0).start()
    for r in range(16):
        tok_copy(r).start()
    acc[...] = jnp.zeros_like(acc)

    @pl.loop(0, 16)
    def _(r):
        slot = r % 2

        @pl.when(r < 15)
        def _():
            kv_copy(r + 1, 1 - slot).start()

        tok_copy(r).wait()
        kv_copy(r, slot).wait()
        acc[:, 0:256] += jnp.dot(tok[r], wkv[slot], preferred_element_type=F32)

    kvs[...] = acc[:, 0:256].astype(BF16)
    acc[...] = jnp.zeros_like(acc)

    most = stretch.shape[1]
    lens = [new_ref[req, j] for j in range(groups)]
    ends = []
    for n in lens:
        ends.append(n if not ends else ends[-1] + n)
    ahead = lax.broadcasted_iota(jnp.int32, (most, count), 1) - lax.broadcasted_iota(jnp.int32, (most, count), 0)
    for d in range(0, groups, 8):
        picks = []
        for dest in range(d, d + 8):
            first = jnp.int32(0)
            for j in range(groups):
                first += jnp.where(route_ref[req, j] == dest, ends[j] - lens[j], 0)
            picks.append(jnp.where(ahead == first, 1.0, 0.0).astype(BF16))
        rows = jnp.dot(jnp.concatenate(picks, axis=0), kvs[...], preferred_element_type=F32)
        outgoing[d:d + 8] = rows.astype(BF16).reshape(8, most, 256)

    def handoff(i):
        to = (req + i) % groups
        return pltpu.make_async_remote_copy(
            src_ref=outgoing.at[to],
            dst_ref=stretch.at[req],
            send_sem=hs.at[i],
            recv_sem=hr.at[i],
            device_id=(tp, to),
            device_id_type=MESH,
        )

    for i in range(1, groups):
        handoff(i).start()
    stretch[req] = outgoing[req]

    def cache_copy(r):
        return pltpu.make_async_copy(cache_hbm.at[:, r], cbuf.at[r % 2], csem.at[r % 2])

    cache_copy(0).start()
    cache_copy(1).start()

    def decode(r):
        if r == 0:
            for i in range(1, groups):
                handoff(i).wait_recv()
        cache_copy(r).wait()
        slot = r % 2
        span = cbuf.shape[2]
        by_head = (((1,), (1,)), ((), ()))
        q = dq_ref[r]
        s = lax.dot_general(q, cbuf[slot, 0], by_head, preferred_element_type=F32) * scale
        col = lax.broadcasted_iota(jnp.int32, (32, span), 1)
        s = jnp.where(col < held_ref[0, r], s, NEG)
        keys = jnp.concatenate([stretch[r, :, 0:128], fresh_ref[r, 0]], axis=0)
        values = jnp.concatenate([stretch[r, :, 128:256], fresh_ref[r, 1]], axis=0)
        t = lax.dot_general(q, keys, by_head, preferred_element_type=F32) * scale
        col = lax.broadcasted_iota(jnp.int32, (32, 2 * most), 1)
        step = lax.broadcasted_iota(jnp.int32, (32, 2 * most), 0) >> 3
        given = jnp.int32(0)
        for j in range(groups):
            given += jnp.where(route_ref[r, j] == req, new_ref[r, j], 0)
        ok = (col < given) | ((col >= most) & (col - most <= step))
        t = jnp.where(ok, t, NEG)
        top = jnp.maximum(jnp.max(s, axis=1, keepdims=True), jnp.max(t, axis=1, keepdims=True))
        w = jnp.exp(s - top)
        f = jnp.exp(t - top)
        total = jnp.sum(w, axis=1, keepdims=True) + jnp.sum(f, axis=1, keepdims=True)
        got = jnp.dot(w.astype(BF16), cbuf[slot, 1], preferred_element_type=F32)
        got += jnp.dot(f.astype(BF16), values, preferred_element_type=F32)
        dec_ref[r] = (got / total).astype(BF16)
        if r + 2 < groups:
            cache_copy(r + 2).start()

    def place(slot):
        return (x + slot[0]) % 4, (yhi + slot[1]) % 2

    def query_unit(unit):
        slot = unit[0][1] * 4 + unit[0][0]
        xs, yhs = place(unit[0])
        start, size = row_range(unit[1], CUT_Q, chunk)
        gq.shared(*unit)

        @pl.loop(0, 8)
        def _(j):
            lane = j // 4
            cols = pl.ds(pl.multiple_of((j % 4) * 256, 256), 256)
            r = yhs * 8 + xs * 2 + c + lane * (1 - 2 * c)
            acc[:, cols] += jnp.dot(
                tok[r, :, start:start + size],
                wq[lane, slot, start:start + size, cols],
                preferred_element_type=F32,
            )

    query_unit(UNITS[0])
    query_unit(UNITS[1])
    waiting = []
    for k in range(len(EVENTS)):
        gq.event(k)
        if k == 1:
            swap_o.start()
        if k == START_O:
            own_o.wait()
            swap_o.wait_recv()
            go.start(START_1)
        if k == START_O + 1:
            go.start(START_2)
        for unit in waiting:
            query_unit(unit)
        waiting = EVENTS[k][2]
        if k >= 1:
            decode(k - 1)
    for unit in waiting:
        query_unit(unit)
    query[...] = acc[...].astype(BF16)

    def swap_mixed(b):
        rows = pl.ds(b * 256, 256)
        return pltpu.make_async_remote_copy(
            src_ref=mixed.at[ylo, rows],
            dst_ref=mixed.at[ylo, rows],
            send_sem=ms.at[b],
            recv_sem=mr.at[b],
            device_id=near["yl"],
            device_id_type=MESH,
        )

    for b in range(4):
        first = max(b - 1, 0) * 128
        rows = slice(b * 128, b * 128 + 128)
        q8 = jnp.concatenate([query[rows, h * 128:h * 128 + 128] for h in range(8)], axis=0)
        keys = kvs[first:first + 256, 0:128]
        values = kvs[first:first + 256, 128:256]
        s = lax.dot_general(q8, keys, (((1,), (1,)), ((), ())), preferred_element_type=F32) * scale
        row = lax.broadcasted_iota(jnp.int32, (128, 1), 0) + b * 128
        col = lax.broadcasted_iota(jnp.int32, (1, 256), 1) + first
        begin = jnp.zeros((128, 1), jnp.int32)
        for n, end in zip(lens, ends):
            begin += jnp.where(row >= end, n, 0)
        bias = jnp.where((col >= begin) & (col <= row), 0.0, NEG)
        s = (s.reshape(8, 128, 256) + bias[None]).reshape(1024, 256)
        w = jnp.exp(s - jnp.max(s, axis=1, keepdims=True))
        total = jnp.sum(w, axis=1, keepdims=True)
        o = jnp.dot(w.astype(BF16), values, preferred_element_type=F32) / total
        o = o.astype(BF16)
        for h in range(8):
            mixed[ylo, rows, h * 128:h * 128 + 128] = o[h * 128:h * 128 + 128]
        if b % 2 == 1:
            swap_mixed(b // 2).start()
        if b >= 1 and b < 3:
            go.event(b - 1)

    def role(slot):
        xs, yhs = place(slot)
        zs = yhs * 2 + xs // 2
        return (z + 4 - zs) % 4, zs, xs % 2

    def item(k):
        source, parts, row, rows = ITEMS[k]
        return source, source[1] * 4 + source[0], row, rows, *row_range(parts, CUT_O, half)

    def z_copy(k, dz):
        source, slot, row, rows, start, size = item(k)
        return pltpu.make_async_remote_copy(
            src_ref=tok.at[pl.ds(2 * slot, 2), pl.ds(row, rows), pl.ds(start, size)],
            dst_ref=rf.at[role(source)[2], dz - 1, :, pl.ds(row, rows), pl.ds(start, size)],
            send_sem=fs.at[k],
            recv_sem=fr.at[k, dz - 1],
            device_id=near["z%d" % (4 - dz)],
            device_id_type=MESH,
        )

    def out_cols(lane, start):
        return pl.multiple_of((c + lane * (1 - 2 * c)) * chunk + e * half + start, 128)

    def y_copy(k, lane):
        source, slot, row, rows, start, size = item(k)
        return pltpu.make_async_remote_copy(
            src_ref=tok.at[2 * slot + lane, pl.ds(row, rows), pl.ds(start, size)],
            dst_ref=out_ref.at[pl.ds(row, rows), pl.ds(out_cols(lane, start), size)],
            send_sem=ys.at[k, lane],
            recv_sem=yr.at[k, lane],
            device_id=near["yl"],
            device_id_type=MESH,
        )

    def part_item(k):
        source, slot, row, rows, start, size = item(k)
        if row == 0:
            go.shared(source, ITEMS[k][1])

        @pl.loop(0, 2)
        def _(lane):
            by_head = (((1,), (1,)), ((), ()))
            total = lax.dot_general(
                mixed[0, row:row + rows],
                wo[lane, slot, 0, start:start + size, :],
                by_head,
                preferred_element_type=F32,
            )
            total += lax.dot_general(
                mixed[1, row:row + rows],
                wo[lane, slot, 1, start:start + size, :],
                by_head,
                preferred_element_type=F32,
            )
            tok[2 * slot + lane, row:row + rows, start:start + size] = total.astype(BF16)

        dz, _, _ = role(source)
        for d in range(1, 4):

            @pl.when(dz == d)
            def _():
                z_copy(k, d).start()

    STEP = 64

    def collect(k):
        source, slot, row, rows, start, size = item(k)
        dz, _, ylos = role(source)

        @pl.when(dz == 0)
        def _():
            for d in range(1, 4):
                z_copy(k, d).wait_recv()

            def summed(j):
                lane = j // (rows // STEP)
                at = pl.ds(pl.multiple_of(row + (j % (rows // STEP)) * STEP, STEP), STEP)
                total = tok[2 * slot + lane, at, start:start + size].astype(F32)
                for d in range(3):
                    total += rf[ylos, d, lane, at, start:start + size].astype(F32)
                return lane, at, total.astype(BF16)

            @pl.when(ylos == ylo)
            def _():
                @pl.loop(0, 2 * (rows // STEP))
                def _(j):
                    lane, at, total = summed(j)
                    out_ref[at, pl.ds(out_cols(lane, start), size)] = total

            @pl.when(ylos != ylo)
            def _():
                @pl.loop(0, 2 * (rows // STEP))
                def _(j):
                    lane, at, total = summed(j)
                    tok[2 * slot + lane, at, start:start + size] = total

                for lane in range(2):
                    y_copy(k, lane).start()

    for what, k in PLAN:
        if what == "mixed":
            swap_mixed(k).wait_recv()
        elif what == "event":
            go.event(k)
        elif what == "part":
            part_item(k)
        elif what == "decode":
            decode(k)
        else:
            collect(k)

    gq.finish()
    go.finish()
    swap_o.wait_send()
    for i in range(1, groups):
        handoff(i).wait_send()
    for b in range(2):
        swap_mixed(b).wait_send()
    for k in range(len(ITEMS)):
        dz, _, ylos = role(ITEMS[k][0])
        for d in range(1, 4):

            @pl.when(dz == d)
            def _():
                z_copy(k, d).wait_send()

        @pl.when((dz == 0) & (ylos != ylo))
        def _():
            for lane in range(2):
                y_copy(k, lane).wait_send()

        @pl.when((dz == 0) & (ylos == ylo))
        def _():
            for lane in range(2):
                y_copy(k, lane).wait_recv()


def layer(tokens, wq, wkv, wo, cache, fresh, decode_query, cache_len, new_len, route):
    count, model = tokens.shape
    requests, most, span = (fresh.shape[0], fresh.shape[2], cache.shape[2])
    rows, cols = wq.shape
    any_ = pl.BlockSpec(memory_space=pl.ANY)
    vmem = pl.BlockSpec(memory_space=pltpu.VMEM)
    smem = pl.BlockSpec(memory_space=pltpu.SMEM)
    dma = pltpu.SemaphoreType.DMA
    n = len(ITEMS)
    return pl.pallas_call(
        layer_kernel,
        name="layer",
        out_shape=(
            jax.ShapeDtypeStruct((count, cols), BF16),
            jax.ShapeDtypeStruct(decode_query.shape, BF16),
        ),
        in_specs=[any_, any_, any_, any_, any_, vmem, vmem, smem, smem, smem],
        out_specs=(vmem, vmem),
        scratch_shapes=[
            pltpu.VMEM((16, count, 512), BF16),
            pltpu.VMEM((2, 8, rows, cols), BF16),
            pltpu.VMEM((2, 8, 2, rows // 2, cols), BF16),
            pltpu.VMEM((count, cols), F32),
            pltpu.VMEM((count, cols), BF16),
            pltpu.VMEM((2, count, cols), BF16),
            pltpu.VMEM((2, 3, 2, count, 256), BF16),
            pltpu.VMEM((2, 512, 256), BF16),
            pltpu.VMEM((count, 256), BF16),
            pltpu.VMEM((requests, most, 256), BF16),
            pltpu.VMEM((requests, most, 256), BF16),
            pltpu.VMEM((2, 2, span, 128), BF16),
            dma((len(MOVES_ALL),)), dma((len(MOVES_ALL),)), dma((len(MOVES_ALL),)), dma((len(MOVES_ALL),)),
            dma((2,)), dma((2,)), dma((1,)), dma((1,)),
            dma((n,)), dma((n, 3)), dma((n, 2)), dma((n, 2)),
            dma((16,)), dma((2,)), dma((2,)), dma((requests,)), dma((requests,)), dma((2,)),
        ],
        compiler_params=pltpu.CompilerParams(
            collective_id=0, has_side_effects=True, vmem_limit_bytes=63 * 2**20
        ),
    )(tokens, wq, wkv, wo, cache, fresh, decode_query, cache_len, new_len, route)


def local(
    tokens, w_query, w_keyval, output_weight, cache, fresh, decode_query, cache_len, new_len, route
):
    count, model = tokens.shape
    slots = route.shape[1]
    steps, rows, qcols = decode_query.shape
    width = w_keyval.shape[2] // 2
    heads = qcols // width
    most = 2 * count // slots
    extra = jnp.pad(jnp.transpose(fresh, (2, 0, 1, 3)), ((0, 0), (0, 0), (0, most - steps), (0, 0)))
    dq = decode_query.reshape(steps, rows, heads, width).transpose(1, 0, 2, 3).reshape(rows, steps * heads, width)
    prefill_out, decoded = layer(
        tokens,
        w_query.reshape(w_query.shape[0], -1),
        w_keyval.reshape(model, -1),
        output_weight.reshape(output_weight.shape[0], -1),
        cache,
        extra,
        dq,
        cache_len,
        new_len,
        route,
    )
    decode_out = decoded.reshape(rows, steps, heads, width).transpose(1, 0, 2, 3).reshape(steps, rows, qcols)
    return (prefill_out, decode_out)


def solution(mesh):
    placed = (
        P("req", None),
        P("req", "tp", None),
        P(None, "tp", None),
        P("req", "tp", None),
        P(None, "req", None, "tp"),
        P(None, None, "req", "tp"),
        P(None, "req", "tp"),
        P("req", None),
        P(),
        P(),
    )
    return jax.shard_map(
        local,
        mesh=mesh,
        in_specs=placed,
        out_specs=(P("req", "tp"), P(None, "req", "tp")),
        check_vma=False,
    )
```

```python
import functools

import jax
import jax.numpy as jnp
from jax import lax
from jax.experimental import pallas as pl
from jax.experimental.pallas import tpu as pltpu
from jax.sharding import PartitionSpec as P

NEG = -1e30
MESH = pl.DeviceIdType.MESH
F32 = jnp.float32
BF16 = jnp.bfloat16

CUT_Q = 384
CUT_O = 128
START_O = 3

MOVES = {
    "yA": ((0, 0), "A", (0, 1), "y"),
    "xpA": ((0, 0), "A", (3, 0), "xp"),
    "xmA": ((0, 0), "A", (1, 0), "xm"),
    "xpB": ((0, 0), "B", (3, 0), "xp"),
    "xmB": ((0, 0), "B", (1, 0), "xm"),
    "xpC": ((0, 1), "A", (3, 1), "xp"),
    "xmC": ((0, 1), "A", (1, 1), "xm"),
    "fpA": ((3, 0), "A0", (2, 0), "xp"),
    "fmA": ((1, 0), "A1", (2, 0), "xm"),
    "fpC": ((3, 1), "A0", (2, 1), "xp"),
    "fmC": ((1, 1), "A1", (2, 1), "xm"),
    "fpB": ((3, 0), "B0", (2, 0), "xp"),
    "fmB": ((1, 0), "B1", (2, 0), "xm"),
    "yB0": ((0, 0), "B", (0, 1), "y"),
    "yBm": ((3, 0), "B", (3, 1), "y"),
    "yBp": ((1, 0), "B", (1, 1), "y"),
    "yB2p": ((2, 0), "B0", (2, 1), "y"),
    "yB2m": ((2, 0), "B1", (2, 1), "y"),
}
FIRST_A = ["yA", "xpA", "xmA", "s00A"]
FIRST_B = ["xpB", "xmB", "yB0", "s00B"]
EVENTS = [
    (["yA"], ["xpC", "xmC", "s01A"], [((0, 1), "A")]),
    (["xpA", "xmA"], ["fpA", "fmA", "s30A", "s10A"], [((3, 0), "A"), ((1, 0), "A")]),
    (["xpB", "xmB"], ["fpB", "fmB", "yBm", "yBp", "s30B", "s10B"], [((3, 0), "B"), ((1, 0), "B")]),
    (["xpC", "xmC"], ["fpC", "fmC", "s31A", "s11A"], [((3, 1), "A"), ((1, 1), "A")]),
    (["fpA", "fmA"], ["s20A"], [((2, 0), "A")]),
    (["fpB", "fmB"], ["yB2p", "yB2m", "s20B"], [((2, 0), "B")]),
    (["yB0"], ["s01B"], [((0, 1), "B")]),
    (["yBm", "yBp"], ["s31B", "s11B"], [((3, 1), "B"), ((1, 1), "B")]),
    (["fpC", "fmC"], ["s21A"], [((2, 1), "A")]),
    (["yB2p", "yB2m"], ["s21B"], [((2, 1), "B")]),
]
UNITS = [((0, 0), "A"), ((0, 0), "B")] + [u for e in EVENTS for u in e[2]]
MOVES_ALL = {**MOVES, **{"s%d%d%s" % (slot + (part,)): (slot, part, slot, "sib") for slot, part in UNITS}}
EVENTS_O = [EVENTS[k] for k in (2, 0, 1, 5, 3, 4, 6, 7, 8, 9)]
START_1 = ["xpB", "xmB", "yA", "s00B"]
START_2 = ["xpA", "xmA", "yB0", "s00A"]
EARLY = [((0, 0), "AB"), ((0, 1), "AB"), ((3, 0), "AB"), ((1, 0), "AB")]
LATE = [((3, 1), "AB"), ((1, 1), "AB"), ((2, 0), "AB"), ((2, 1), "A"), ((2, 1), "B")]
ITEMS = [e + (r, 256) for r in (0, 256) for e in EARLY] + [e + (0, 512) for e in LATE]


def span(what, first, last):
    return [(what, k) for k in range(first, last)]


PLAN = (
    [("event", 2), ("event", 6), ("mixed", 0)] + span("part", 0, 2) + [("event", 3)] + span("part", 2, 4) + [("mixed", 1)]
    + span("pass", 0, 2) + span("part", 4, 8) + span("pass", 2, 4) + [("event", 4), ("event", 7)] + span("pass", 4, 6)
    + span("part", 8, 10) + span("pass", 6, 8) + [("event", 5), ("part", 10)] + span("pass", 8, 10)
    + span("collect", 0, 8) + [("event", 8), ("part", 11), ("pass", 10), ("event", 9), ("part", 12)]
    + span("pass", 11, 13) + span("decode", 9, 16) + span("collect", 8, 13)
)


def where_am_i():
    tp = lax.axis_index("tp")
    req = lax.axis_index("req")
    return tp // 2, tp % 2, req // 8, (req // 2) % 4, req % 2


def neighbours():
    z, ylo, yhi, x, c = where_am_i()
    tp = z * 2 + ylo
    req = yhi * 8 + x * 2 + c
    return {
        "xp": (tp, yhi * 8 + ((x + 1) % 4) * 2 + c),
        "xm": (tp, yhi * 8 + ((x + 3) % 4) * 2 + c),
        "y": (tp, (1 - yhi) * 8 + x * 2 + c),
        "y3": (z * 2 + (1 - ylo), (1 - yhi) * 8 + x * 2 + c),
        "sib": (tp, yhi * 8 + x * 2 + (1 - c)),
        "z1": (((z + 1) % 4) * 2 + ylo, req),
        "z2": (((z + 2) % 4) * 2 + ylo, req),
        "z3": (((z + 3) % 4) * 2 + ylo, req),
        "yl": (z * 2 + (1 - ylo), req),
    }


def row_range(part, cut, rows):
    rest = rows - cut
    return {
        "A": (0, cut),
        "A0": (0, cut // 2),
        "A1": (cut // 2, cut // 2),
        "B": (cut, rest),
        "B0": (cut, rest // 2),
        "B1": (cut + rest // 2, rest // 2),
        "AB": (0, rows),
    }[part]


class Gather:
    def __init__(self, view, events, rows, cut, send, recv, near):
        self.view, self.moves, self.events = view, MOVES_ALL, events
        self.rows, self.cut, self.send, self.recv, self.near = rows, cut, send, recv, near
        self.index = {name: i for i, name in enumerate(MOVES_ALL)}

    def copy(self, name):
        src, part, dst, way = self.moves[name]
        start, size = row_range(part, self.cut, self.rows)
        lane = 1 if way == "sib" else 0
        i = self.index[name]
        return pltpu.make_async_remote_copy(
            src_ref=self.view(0, src[1] * 4 + src[0], pl.ds(start, size)),
            dst_ref=self.view(lane, dst[1] * 4 + dst[0], pl.ds(start, size)),
            send_sem=self.send.at[i],
            recv_sem=self.recv.at[i],
            device_id=self.near[way],
            device_id_type=MESH,
        )

    def start(self, names):
        for name in names:
            self.copy(name).start()

    def event(self, k):
        waits, starts, _ = self.events[k]
        for name in waits:
            self.copy(name).wait_recv()
        self.start(starts)

    def shared(self, slot, parts):
        for part in parts:
            self.copy("s%d%d%s" % (slot + (part,))).wait_recv()

    def finish(self):
        for name in self.moves:
            self.copy(name).wait_send()


def layer_kernel(
    tok_hbm, wq_hbm, wkv_hbm, wo_hbm, cache_hbm, fresh_ref, dq_ref, held_ref, new_ref, route_ref,
    out_ref, dec_ref,
    tok, wq, wo, acc, query, mixed, rh, rf, wkv, kvs, outgoing, stretch, cbuf,
    qs, qr, os_, or_, ms, mr, ps, pr, hs2, hr2, fs, fr, ys, yr, tsem, ksem, lsem, hs, hr, csem,
):
    z, ylo, yhi, x, c = where_am_i()
    near = neighbours()
    count = tok.shape[1]
    chunk = tok.shape[2]
    half = chunk // 2
    scale = 128 ** -0.5

    e = (ylo + yhi) % 2
    own_half = pl.ds(pl.multiple_of(e * half, half), half)
    other_half = pl.ds(pl.multiple_of((1 - e) * half, half), half)
    own_q = pltpu.make_async_copy(wq_hbm, wq.at[0, 0], lsem.at[0])
    own_o = pltpu.make_async_copy(wo_hbm.at[own_half], wo.at[0, 0, ylo], lsem.at[1])
    own_q.start()
    own_o.start()

    tp = z * 2 + ylo
    req = yhi * 8 + x * 2 + c
    groups = stretch.shape[0]
    barrier = pltpu.get_barrier_semaphore()
    for way in ("z1", "z3", "yl", "y3"):
        pl.semaphore_signal(barrier, inc=1, device_id=near[way], device_id_type=MESH)
    for i in range(1, groups):
        pl.semaphore_signal(barrier, inc=1, device_id=(tp, (req + i) % groups), device_id_type=MESH)
    pl.semaphore_wait(barrier, 4 + groups - 1)

    gq = Gather(lambda lane, slot, rows: wq.at[lane, slot, rows], EVENTS, chunk, CUT_Q, qs, qr, near)
    go = Gather(
        lambda lane, slot, rows: wo.at[lane, slot, :, rows], EVENTS_O, half, CUT_O, os_, or_, {**near, "y": near["y3"]}
    )
    swap_o = pltpu.make_async_remote_copy(
        src_ref=wo_hbm.at[other_half],
        dst_ref=wo.at[0, 0, ylo],
        send_sem=ps.at[0],
        recv_sem=pr.at[0],
        device_id=near["yl"],
        device_id_type=MESH,
    )
    own_q.wait()
    gq.start(FIRST_A)
    gq.start(FIRST_B)

    def tok_copy(r):
        return pltpu.make_async_copy(tok_hbm.at[:, pl.ds(r * chunk, chunk)], tok.at[r], tsem.at[r])

    def kv_copy(r, slot):
        return pltpu.make_async_copy(wkv_hbm.at[pl.ds(r * chunk, chunk)], wkv.at[slot], ksem.at[slot])

    kv_copy(0, 0).start()
    for r in range(16):
        tok_copy(r).start()
    acc[...] = jnp.zeros_like(acc)

    @pl.loop(0, 16)
    def _(r):
        slot = r % 2

        @pl.when(r < 15)
        def _():
            kv_copy(r + 1, 1 - slot).start()

        tok_copy(r).wait()
        kv_copy(r, slot).wait()
        acc[:, 0:256] += jnp.dot(tok[r], wkv[slot], preferred_element_type=F32)

    kvs[...] = acc[:, 0:256].astype(BF16)
    acc[...] = jnp.zeros_like(acc)

    most = stretch.shape[1]
    lens = [new_ref[req, j] for j in range(groups)]
    ends = []
    for n in lens:
        ends.append(n if not ends else ends[-1] + n)
    ahead = lax.broadcasted_iota(jnp.int32, (most, count), 1) - lax.broadcasted_iota(jnp.int32, (most, count), 0)
    for d in range(0, groups, 8):
        picks = []
        for dest in range(d, d + 8):
            first = jnp.int32(0)
            for j in range(groups):
                first += jnp.where(route_ref[req, j] == dest, ends[j] - lens[j], 0)
            picks.append(jnp.where(ahead == first, 1.0, 0.0).astype(BF16))
        rows = jnp.dot(jnp.concatenate(picks, axis=0), kvs[...], preferred_element_type=F32)
        outgoing[d:d + 8] = rows.astype(BF16).reshape(8, most, 256)

    def handoff(i):
        to = (req + i) % groups
        return pltpu.make_async_remote_copy(
            src_ref=outgoing.at[to],
            dst_ref=stretch.at[req],
            send_sem=hs.at[i],
            recv_sem=hr.at[i],
            device_id=(tp, to),
            device_id_type=MESH,
        )

    for i in range(1, groups):
        handoff(i).start()
    stretch[req] = outgoing[req]

    def cache_copy(r):
        return pltpu.make_async_copy(cache_hbm.at[:, r], cbuf.at[r % 2], csem.at[r % 2])

    cache_copy(0).start()
    cache_copy(1).start()

    def decode(r):
        if r == 0:
            for i in range(1, groups):
                handoff(i).wait_recv()
        cache_copy(r).wait()
        slot = r % 2
        span = cbuf.shape[2]
        by_head = (((1,), (1,)), ((), ()))
        q = dq_ref[r]
        s = lax.dot_general(q, cbuf[slot, 0], by_head, preferred_element_type=F32) * scale
        col = lax.broadcasted_iota(jnp.int32, (32, span), 1)
        s = jnp.where(col < held_ref[0, r], s, NEG)
        keys = jnp.concatenate([stretch[r, :, 0:128], fresh_ref[r, 0]], axis=0)
        values = jnp.concatenate([stretch[r, :, 128:256], fresh_ref[r, 1]], axis=0)
        t = lax.dot_general(q, keys, by_head, preferred_element_type=F32) * scale
        col = lax.broadcasted_iota(jnp.int32, (32, 2 * most), 1)
        step = lax.broadcasted_iota(jnp.int32, (32, 2 * most), 0) >> 3
        given = jnp.int32(0)
        for j in range(groups):
            given += jnp.where(route_ref[r, j] == req, new_ref[r, j], 0)
        ok = (col < given) | ((col >= most) & (col - most <= step))
        t = jnp.where(ok, t, NEG)
        top = jnp.maximum(jnp.max(s, axis=1, keepdims=True), jnp.max(t, axis=1, keepdims=True))
        w = jnp.exp(s - top)
        f = jnp.exp(t - top)
        total = jnp.sum(w, axis=1, keepdims=True) + jnp.sum(f, axis=1, keepdims=True)
        got = jnp.dot(w.astype(BF16), cbuf[slot, 1], preferred_element_type=F32)
        got += jnp.dot(f.astype(BF16), values, preferred_element_type=F32)
        dec_ref[r] = (got / total).astype(BF16)
        if r + 2 < groups:
            cache_copy(r + 2).start()

    def place(slot):
        return (x + slot[0]) % 4, (yhi + slot[1]) % 2

    def query_unit(unit):
        slot = unit[0][1] * 4 + unit[0][0]
        xs, yhs = place(unit[0])
        start, size = row_range(unit[1], CUT_Q, chunk)
        gq.shared(*unit)

        @pl.loop(0, 8)
        def _(j):
            lane = j // 4
            cols = pl.ds(pl.multiple_of((j % 4) * 256, 256), 256)
            r = yhs * 8 + xs * 2 + c + lane * (1 - 2 * c)
            acc[:, cols] += jnp.dot(
                tok[r, :, start:start + size],
                wq[lane, slot, start:start + size, cols],
                preferred_element_type=F32,
            )

    query_unit(UNITS[0])
    query_unit(UNITS[1])
    waiting = []
    for k in range(len(EVENTS)):
        gq.event(k)
        if k == 1:
            swap_o.start()
        if k == START_O:
            own_o.wait()
            swap_o.wait_recv()
            go.start(START_1)
        if k == START_O + 1:
            go.start(START_2)
        for unit in waiting:
            query_unit(unit)
        waiting = EVENTS[k][2]
        if k >= 1:
            decode(k - 1)
    for unit in waiting:
        query_unit(unit)
    query[...] = acc[...].astype(BF16)

    def swap_mixed(b):
        rows = pl.ds(b * 256, 256)
        return pltpu.make_async_remote_copy(
            src_ref=mixed.at[ylo, rows],
            dst_ref=mixed.at[ylo, rows],
            send_sem=ms.at[b],
            recv_sem=mr.at[b],
            device_id=near["yl"],
            device_id_type=MESH,
        )

    for b in range(4):
        first = max(b - 1, 0) * 128
        rows = slice(b * 128, b * 128 + 128)
        q8 = jnp.concatenate([query[rows, h * 128:h * 128 + 128] for h in range(8)], axis=0)
        keys = kvs[first:first + 256, 0:128]
        values = kvs[first:first + 256, 128:256]
        s = lax.dot_general(q8, keys, (((1,), (1,)), ((), ())), preferred_element_type=F32) * scale
        row = lax.broadcasted_iota(jnp.int32, (128, 1), 0) + b * 128
        col = lax.broadcasted_iota(jnp.int32, (1, 256), 1) + first
        begin = jnp.zeros((128, 1), jnp.int32)
        for n, end in zip(lens, ends):
            begin += jnp.where(row >= end, n, 0)
        bias = jnp.where((col >= begin) & (col <= row), 0.0, NEG)
        s = (s.reshape(8, 128, 256) + bias[None]).reshape(1024, 256)
        w = jnp.exp(s - jnp.max(s, axis=1, keepdims=True))
        total = jnp.sum(w, axis=1, keepdims=True)
        o = jnp.dot(w.astype(BF16), values, preferred_element_type=F32) / total
        o = o.astype(BF16)
        for h in range(8):
            mixed[ylo, rows, h * 128:h * 128 + 128] = o[h * 128:h * 128 + 128]
        if b % 2 == 1:
            swap_mixed(b // 2).start()
        if b >= 1 and b < 3:
            go.event(b - 1)

    def role(slot):
        xs, yhs = place(slot)
        zs = yhs * 2 + xs // 2
        return (z + 4 - zs) % 4, zs, xs % 2

    def item(k):
        source, parts, row, rows = ITEMS[k]
        return source, source[1] * 4 + source[0], row, rows, *row_range(parts, CUT_O, half)

    def far_copy(k, which):
        source, slot, row, rows, start, size = item(k)
        return pltpu.make_async_remote_copy(
            src_ref=tok.at[pl.ds(2 * slot, 2), pl.ds(row + which * (rows // 2), rows // 2), pl.ds(start, size)],
            dst_ref=rh.at[slot, :, pl.ds(row // 2, rows // 2), pl.ds(start, size)],
            send_sem=hs2.at[k, which],
            recv_sem=hr2.at[k, which],
            device_id=near["z3" if which else "z1"],
            device_id_type=MESH,
        )

    def near_copy(k, which, part):
        source, slot, row, rows, start, size = item(k)
        at = pl.ds(row + part * (rows // 2), rows // 2)
        return pltpu.make_async_remote_copy(
            src_ref=tok.at[pl.ds(2 * slot, 2), at, pl.ds(start, size)],
            dst_ref=rf.at[role(source)[2], which, :, at, pl.ds(start, size)],
            send_sem=fs.at[k, part],
            recv_sem=fr.at[k, which * 2 + part],
            device_id=near["z3" if which else "z1"],
            device_id_type=MESH,
        )

    def out_cols(lane, start):
        return pl.multiple_of((c + lane * (1 - 2 * c)) * chunk + e * half + start, 128)

    def y_copy(k, lane):
        source, slot, row, rows, start, size = item(k)
        return pltpu.make_async_remote_copy(
            src_ref=tok.at[2 * slot + lane, pl.ds(row, rows), pl.ds(start, size)],
            dst_ref=out_ref.at[pl.ds(row, rows), pl.ds(out_cols(lane, start), size)],
            send_sem=ys.at[k, lane],
            recv_sem=yr.at[k, lane],
            device_id=near["yl"],
            device_id_type=MESH,
        )

    def part_item(k):
        source, slot, row, rows, start, size = item(k)
        if row == 0:
            go.shared(source, ITEMS[k][1])

        @pl.loop(0, 2)
        def _(lane):
            by_head = (((1,), (1,)), ((), ()))
            total = lax.dot_general(
                mixed[0, row:row + rows],
                wo[lane, slot, 0, start:start + size, :],
                by_head,
                preferred_element_type=F32,
            )
            total += lax.dot_general(
                mixed[1, row:row + rows],
                wo[lane, slot, 1, start:start + size, :],
                by_head,
                preferred_element_type=F32,
            )
            tok[2 * slot + lane, row:row + rows, start:start + size] = total.astype(BF16)

        dz, _, _ = role(source)

        @pl.when(dz == 2)
        def _():
            far_copy(k, 0).start()
            far_copy(k, 1).start()

        for which in range(2):

            @pl.when(dz == (1 if which else 3))
            def _():
                near_copy(k, which, 1 - which).start()

    STEP = 64

    def pass_on(k):
        source, slot, row, rows, start, size = item(k)
        dz, _, _ = role(source)
        for which in range(2):

            @pl.when(dz == (1 if which else 3))
            def _():
                far_copy(k, which).wait_recv()
                steps = rows // 2 // STEP

                @pl.loop(0, 2 * steps)
                def _(j):
                    lane = j // steps
                    i = pl.multiple_of((j % steps) * STEP, STEP)
                    at = pl.ds(row + which * (rows // 2) + i, STEP)
                    total = tok[2 * slot + lane, at, start:start + size].astype(F32)
                    total += rh[slot, lane, pl.ds(row // 2 + i, STEP), start:start + size].astype(F32)
                    tok[2 * slot + lane, at, start:start + size] = total.astype(BF16)

                near_copy(k, which, which).start()

    def collect(k):
        source, slot, row, rows, start, size = item(k)
        dz, _, ylos = role(source)

        @pl.when(dz == 0)
        def _():
            for which in range(2):
                for part in range(2):
                    near_copy(k, which, part).wait_recv()

            def summed(j):
                lane = j // (rows // STEP)
                at = pl.ds(pl.multiple_of(row + (j % (rows // STEP)) * STEP, STEP), STEP)
                total = tok[2 * slot + lane, at, start:start + size].astype(F32)
                for d in range(2):
                    total += rf[ylos, d, lane, at, start:start + size].astype(F32)
                return lane, at, total.astype(BF16)

            @pl.when(ylos == ylo)
            def _():
                @pl.loop(0, 2 * (rows // STEP))
                def _(j):
                    lane, at, total = summed(j)
                    out_ref[at, pl.ds(out_cols(lane, start), size)] = total

            @pl.when(ylos != ylo)
            def _():
                @pl.loop(0, 2 * (rows // STEP))
                def _(j):
                    lane, at, total = summed(j)
                    tok[2 * slot + lane, at, start:start + size] = total

                for lane in range(2):
                    y_copy(k, lane).start()

    for what, k in PLAN:
        if what == "mixed":
            swap_mixed(k).wait_recv()
        elif what == "event":
            go.event(k)
        elif what == "part":
            part_item(k)
        elif what == "pass":
            pass_on(k)
        elif what == "decode":
            decode(k)
        else:
            collect(k)

    gq.finish()
    go.finish()
    swap_o.wait_send()
    for i in range(1, groups):
        handoff(i).wait_send()
    for b in range(2):
        swap_mixed(b).wait_send()
    for k in range(len(ITEMS)):
        dz, _, ylos = role(ITEMS[k][0])

        @pl.when(dz == 2)
        def _():
            far_copy(k, 0).wait_send()
            far_copy(k, 1).wait_send()

        for which in range(2):

            @pl.when(dz == (1 if which else 3))
            def _():
                near_copy(k, which, 0).wait_send()
                near_copy(k, which, 1).wait_send()

        @pl.when((dz == 0) & (ylos != ylo))
        def _():
            for lane in range(2):
                y_copy(k, lane).wait_send()

        @pl.when((dz == 0) & (ylos == ylo))
        def _():
            for lane in range(2):
                y_copy(k, lane).wait_recv()


def layer(tokens, wq, wkv, wo, cache, fresh, decode_query, cache_len, new_len, route):
    count, model = tokens.shape
    requests, most, span = (fresh.shape[0], fresh.shape[2], cache.shape[2])
    rows, cols = wq.shape
    any_ = pl.BlockSpec(memory_space=pl.ANY)
    vmem = pl.BlockSpec(memory_space=pltpu.VMEM)
    smem = pl.BlockSpec(memory_space=pltpu.SMEM)
    dma = pltpu.SemaphoreType.DMA
    n = len(ITEMS)
    return pl.pallas_call(
        layer_kernel,
        name="layer",
        out_shape=(
            jax.ShapeDtypeStruct((count, cols), BF16),
            jax.ShapeDtypeStruct(decode_query.shape, BF16),
        ),
        in_specs=[any_, any_, any_, any_, any_, vmem, vmem, smem, smem, smem],
        out_specs=(vmem, vmem),
        scratch_shapes=[
            pltpu.VMEM((16, count, 512), BF16),
            pltpu.VMEM((2, 8, rows, cols), BF16),
            pltpu.VMEM((2, 8, 2, rows // 2, cols), BF16),
            pltpu.VMEM((count, cols), F32),
            pltpu.VMEM((count, cols), BF16),
            pltpu.VMEM((2, count, cols), BF16),
            pltpu.VMEM((8, 2, count // 2, 256), BF16),
            pltpu.VMEM((2, 2, 2, count, 256), BF16),
            pltpu.VMEM((2, 512, 256), BF16),
            pltpu.VMEM((count, 256), BF16),
            pltpu.VMEM((requests, most, 256), BF16),
            pltpu.VMEM((requests, most, 256), BF16),
            pltpu.VMEM((2, 2, span, 128), BF16),
            dma((len(MOVES_ALL),)), dma((len(MOVES_ALL),)), dma((len(MOVES_ALL),)), dma((len(MOVES_ALL),)),
            dma((2,)), dma((2,)), dma((1,)), dma((1,)),
            dma((n, 2)), dma((n, 2)), dma((n, 2)), dma((n, 4)), dma((n, 2)), dma((n, 2)),
            dma((16,)), dma((2,)), dma((2,)), dma((requests,)), dma((requests,)), dma((2,)),
        ],
        compiler_params=pltpu.CompilerParams(
            collective_id=0, has_side_effects=True, vmem_limit_bytes=63 * 2**20
        ),
    )(tokens, wq, wkv, wo, cache, fresh, decode_query, cache_len, new_len, route)


def local(
    tokens, w_query, w_keyval, output_weight, cache, fresh, decode_query, cache_len, new_len, route
):
    count, model = tokens.shape
    slots = route.shape[1]
    steps, rows, qcols = decode_query.shape
    width = w_keyval.shape[2] // 2
    heads = qcols // width
    most = 2 * count // slots
    extra = jnp.pad(jnp.transpose(fresh, (2, 0, 1, 3)), ((0, 0), (0, 0), (0, most - steps), (0, 0)))
    dq = decode_query.reshape(steps, rows, heads, width).transpose(1, 0, 2, 3).reshape(rows, steps * heads, width)
    prefill_out, decoded = layer(
        tokens,
        w_query.reshape(w_query.shape[0], -1),
        w_keyval.reshape(model, -1),
        output_weight.reshape(output_weight.shape[0], -1),
        cache,
        extra,
        dq,
        cache_len,
        new_len,
        route,
    )
    decode_out = decoded.reshape(rows, steps, heads, width).transpose(1, 0, 2, 3).reshape(steps, rows, qcols)
    return (prefill_out, decode_out)


def solution(mesh):
    placed = (
        P("req", None),
        P("req", "tp", None),
        P(None, "tp", None),
        P("req", "tp", None),
        P(None, "req", None, "tp"),
        P(None, None, "req", "tp"),
        P(None, "req", "tp"),
        P("req", None),
        P(),
        P(),
    )
    return jax.shard_map(
        local,
        mesh=mesh,
        in_specs=placed,
        out_specs=(P("req", "tp"), P(None, "req", "tp")),
        check_vma=False,
    )
```

```python
import functools

import jax
import jax.numpy as jnp
from jax import lax
from jax.experimental import pallas as pl
from jax.experimental.pallas import tpu as pltpu
from jax.sharding import PartitionSpec as P

NEG = -1e30
MESH = pl.DeviceIdType.MESH
F32 = jnp.float32
BF16 = jnp.bfloat16

CUT_Q = 384
CUT_O = 128
START_O = 3

MOVES = {
    "yA": ((0, 0), "A", (0, 1), "y"),
    "xpA": ((0, 0), "A", (3, 0), "xp"),
    "xmA": ((0, 0), "A", (1, 0), "xm"),
    "xpB": ((0, 0), "B", (3, 0), "xp"),
    "xmB": ((0, 0), "B", (1, 0), "xm"),
    "xpC": ((0, 1), "A", (3, 1), "xp"),
    "xmC": ((0, 1), "A", (1, 1), "xm"),
    "fpA": ((3, 0), "A0", (2, 0), "xp"),
    "fmA": ((1, 0), "A1", (2, 0), "xm"),
    "fpC": ((3, 1), "A0", (2, 1), "xp"),
    "fmC": ((1, 1), "A1", (2, 1), "xm"),
    "fpB": ((3, 0), "B0", (2, 0), "xp"),
    "fmB": ((1, 0), "B1", (2, 0), "xm"),
    "yB0": ((0, 0), "B", (0, 1), "y"),
    "yBm": ((3, 0), "B", (3, 1), "y"),
    "yBp": ((1, 0), "B", (1, 1), "y"),
    "yB2p": ((2, 0), "B0", (2, 1), "y"),
    "yB2m": ((2, 0), "B1", (2, 1), "y"),
}
FIRST_A = ["yA", "xpA", "xmA", "s00A"]
FIRST_B = ["xpB", "xmB", "yB0", "s00B"]
EVENTS = [
    (["yA"], ["xpC", "xmC", "s01A"], [((0, 1), "A")]),
    (["xpA", "xmA"], ["fpA", "fmA", "s30A", "s10A"], [((3, 0), "A"), ((1, 0), "A")]),
    (["xpB", "xmB"], ["fpB", "fmB", "yBm", "yBp", "s30B", "s10B"], [((3, 0), "B"), ((1, 0), "B")]),
    (["xpC", "xmC"], ["fpC", "fmC", "s31A", "s11A"], [((3, 1), "A"), ((1, 1), "A")]),
    (["fpA", "fmA"], ["s20A"], [((2, 0), "A")]),
    (["fpB", "fmB"], ["yB2p", "yB2m", "s20B"], [((2, 0), "B")]),
    (["yB0"], ["s01B"], [((0, 1), "B")]),
    (["yBm", "yBp"], ["s31B", "s11B"], [((3, 1), "B"), ((1, 1), "B")]),
    (["fpC", "fmC"], ["s21A"], [((2, 1), "A")]),
    (["yB2p", "yB2m"], ["s21B"], [((2, 1), "B")]),
]
UNITS = [((0, 0), "A"), ((0, 0), "B")] + [u for e in EVENTS for u in e[2]]
MOVES_ALL = {**MOVES, **{"s%d%d%s" % (slot + (part,)): (slot, part, slot, "sib") for slot, part in UNITS}}
EVENTS_O = [EVENTS[k] for k in (2, 0, 1, 5, 3, 4, 6, 7, 8, 9)]
START_1 = ["xpB", "xmB", "yA", "s00B"]
START_2 = ["xpA", "xmA", "yB0", "s00A"]
EARLY = [((0, 0), "AB"), ((0, 1), "AB"), ((3, 0), "AB"), ((1, 0), "AB")]
LATE = [((3, 1), "AB"), ((1, 1), "AB"), ((2, 0), "AB"), ((2, 1), "A"), ((2, 1), "B")]
ITEMS = [e + (r, 256) for r in (0, 256) for e in EARLY] + [e + (0, 512) for e in LATE]


def span(what, first, last):
    return [(what, k) for k in range(first, last)]


PLAN = (
    [("event", 2), ("event", 6), ("mixed", 0)] + span("part", 0, 2) + [("event", 3)] + span("part", 2, 4) + [("mixed", 1)]
    + span("pass", 0, 2) + span("part", 4, 8) + span("pass", 2, 4) + [("event", 4), ("event", 7)] + span("pass", 4, 6)
    + span("part", 8, 10) + span("pass", 6, 8) + [("event", 5), ("part", 10)] + span("pass", 8, 10)
    + span("collect", 0, 8) + [("event", 8), ("part", 11), ("pass", 10), ("event", 9), ("part", 12)]
    + span("pass", 11, 13) + span("decode", 9, 16) + span("collect", 8, 13)
)


def where_am_i():
    tp = lax.axis_index("tp")
    req = lax.axis_index("req")
    return tp // 2, tp % 2, req // 8, (req // 2) % 4, req % 2


def neighbours():
    z, ylo, yhi, x, c = where_am_i()
    tp = z * 2 + ylo
    req = yhi * 8 + x * 2 + c
    return {
        "xp": (tp, yhi * 8 + ((x + 1) % 4) * 2 + c),
        "xm": (tp, yhi * 8 + ((x + 3) % 4) * 2 + c),
        "y": (tp, (1 - yhi) * 8 + x * 2 + c),
        "y3": (z * 2 + (1 - ylo), (1 - yhi) * 8 + x * 2 + c),
        "sib": (tp, yhi * 8 + x * 2 + (1 - c)),
        "z1": (((z + 1) % 4) * 2 + ylo, req),
        "z2": (((z + 2) % 4) * 2 + ylo, req),
        "z3": (((z + 3) % 4) * 2 + ylo, req),
        "yl": (z * 2 + (1 - ylo), req),
    }


def row_range(part, cut, rows):
    rest = rows - cut
    return {
        "A": (0, cut),
        "A0": (0, cut // 2),
        "A1": (cut // 2, cut // 2),
        "B": (cut, rest),
        "B0": (cut, rest // 2),
        "B1": (cut + rest // 2, rest // 2),
        "AB": (0, rows),
    }[part]


class Gather:
    def __init__(self, view, events, rows, cut, send, recv, near):
        self.view, self.moves, self.events = view, MOVES_ALL, events
        self.rows, self.cut, self.send, self.recv, self.near = rows, cut, send, recv, near
        self.index = {name: i for i, name in enumerate(MOVES_ALL)}

    def copy(self, name):
        src, part, dst, way = self.moves[name]
        start, size = row_range(part, self.cut, self.rows)
        lane = 1 if way == "sib" else 0
        i = self.index[name]
        return pltpu.make_async_remote_copy(
            src_ref=self.view(0, src[1] * 4 + src[0], pl.ds(start, size)),
            dst_ref=self.view(lane, dst[1] * 4 + dst[0], pl.ds(start, size)),
            send_sem=self.send.at[i],
            recv_sem=self.recv.at[i],
            device_id=self.near[way],
            device_id_type=MESH,
        )

    def start(self, names):
        for name in names:
            self.copy(name).start()

    def event(self, k):
        waits, starts, _ = self.events[k]
        for name in waits:
            self.copy(name).wait_recv()
        self.start(starts)

    def shared(self, slot, parts):
        for part in parts:
            self.copy("s%d%d%s" % (slot + (part,))).wait_recv()

    def finish(self):
        for name in self.moves:
            self.copy(name).wait_send()


def layer_kernel(
    tok_hbm, wq_hbm, wkv_hbm, wo_hbm, cache_hbm, fresh_ref, dq_ref, held_ref, new_ref, route_ref,
    out_ref, dec_ref,
    tok, wq, wo, acc, query, mixed, rh, rf, wkv, kvs, outgoing, stretch, cbuf, dec,
    qs, qr, os_, or_, ms, mr, ps, pr, hs2, hr2, fs, fr, ys, yr, tsem, ksem, lsem, hs, hr, csem,
):
    z, ylo, yhi, x, c = where_am_i()
    near = neighbours()
    count = tok.shape[1]
    chunk = tok.shape[2]
    half = chunk // 2
    scale = 128 ** -0.5

    e = (ylo + yhi) % 2
    own_half = pl.ds(pl.multiple_of(e * half, half), half)
    other_half = pl.ds(pl.multiple_of((1 - e) * half, half), half)
    own_q = pltpu.make_async_copy(wq_hbm, wq.at[0, 0], lsem.at[0])
    own_o = pltpu.make_async_copy(wo_hbm.at[own_half], wo.at[0, 0, ylo], lsem.at[1])
    own_q.start()
    own_o.start()

    tp = z * 2 + ylo
    req = yhi * 8 + x * 2 + c
    groups = stretch.shape[0]
    barrier = pltpu.get_barrier_semaphore()
    for way in ("z1", "z3", "yl", "y3"):
        pl.semaphore_signal(barrier, inc=1, device_id=near[way], device_id_type=MESH)
    for i in range(1, groups):
        pl.semaphore_signal(barrier, inc=1, device_id=(tp, (req + i) % groups), device_id_type=MESH)
    pl.semaphore_wait(barrier, 4 + groups - 1)

    gq = Gather(lambda lane, slot, rows: wq.at[lane, slot, rows], EVENTS, chunk, CUT_Q, qs, qr, near)
    go = Gather(
        lambda lane, slot, rows: wo.at[lane, slot, :, rows], EVENTS_O, half, CUT_O, os_, or_, {**near, "y": near["y3"]}
    )
    swap_o = pltpu.make_async_remote_copy(
        src_ref=wo_hbm.at[other_half],
        dst_ref=wo.at[0, 0, ylo],
        send_sem=ps.at[0],
        recv_sem=pr.at[0],
        device_id=near["yl"],
        device_id_type=MESH,
    )
    own_q.wait()
    gq.start(FIRST_A)
    gq.start(FIRST_B)

    def tok_copy(r):
        return pltpu.make_async_copy(tok_hbm.at[:, pl.ds(r * chunk, chunk)], tok.at[r], tsem.at[r])

    def kv_copy(r, slot):
        return pltpu.make_async_copy(wkv_hbm.at[pl.ds(r * chunk, chunk)], wkv.at[slot], ksem.at[slot])

    kv_copy(0, 0).start()
    for r in range(16):
        tok_copy(r).start()
    acc[...] = jnp.zeros_like(acc)

    @pl.loop(0, 16)
    def _(r):
        slot = r % 2

        @pl.when(r < 15)
        def _():
            kv_copy(r + 1, 1 - slot).start()

        tok_copy(r).wait()
        kv_copy(r, slot).wait()
        acc[:, 0:256] += jnp.dot(tok[r], wkv[slot], preferred_element_type=F32)

    kvs[...] = acc[:, 0:256].astype(BF16)
    acc[...] = jnp.zeros_like(acc)

    most = stretch.shape[1]
    lens = [new_ref[req, j] for j in range(groups)]
    ends = []
    for n in lens:
        ends.append(n if not ends else ends[-1] + n)
    ahead = lax.broadcasted_iota(jnp.int32, (most, count), 1) - lax.broadcasted_iota(jnp.int32, (most, count), 0)
    for d in range(0, groups, 8):
        picks = []
        for dest in range(d, d + 8):
            first = jnp.int32(0)
            for j in range(groups):
                first += jnp.where(route_ref[req, j] == dest, ends[j] - lens[j], 0)
            picks.append(jnp.where(ahead == first, 1.0, 0.0).astype(BF16))
        rows = jnp.dot(jnp.concatenate(picks, axis=0), kvs[...], preferred_element_type=F32)
        outgoing[d:d + 8] = rows.astype(BF16).reshape(8, most, 256)

    def handoff(i):
        to = (req + i) % groups
        return pltpu.make_async_remote_copy(
            src_ref=outgoing.at[to],
            dst_ref=stretch.at[req],
            send_sem=hs.at[i],
            recv_sem=hr.at[i],
            device_id=(tp, to),
            device_id_type=MESH,
        )

    for i in range(1, groups):
        handoff(i).start()
    stretch[req] = outgoing[req]

    def cache_copy(r):
        return pltpu.make_async_copy(cache_hbm.at[:, r], cbuf.at[r % 2], csem.at[r % 2])

    cache_copy(0).start()
    cache_copy(1).start()

    def decode(r):
        if r == 0:
            for i in range(1, groups):
                handoff(i).wait_recv()
        cache_copy(r).wait()
        slot = r % 2
        span = cbuf.shape[2]
        by_head = (((1,), (1,)), ((), ()))
        q = dq_ref[r]
        s = lax.dot_general(q, cbuf[slot, 0], by_head, preferred_element_type=F32) * scale
        col = lax.broadcasted_iota(jnp.int32, (32, span), 1)
        s = jnp.where(col < held_ref[0, r], s, NEG)
        keys = jnp.concatenate([stretch[r, :, 0:128], fresh_ref[r, 0]], axis=0)
        values = jnp.concatenate([stretch[r, :, 128:256], fresh_ref[r, 1]], axis=0)
        t = lax.dot_general(q, keys, by_head, preferred_element_type=F32) * scale
        col = lax.broadcasted_iota(jnp.int32, (32, 2 * most), 1)
        step = lax.broadcasted_iota(jnp.int32, (32, 2 * most), 0) >> 3
        given = jnp.int32(0)
        for j in range(groups):
            given += jnp.where(route_ref[r, j] == req, new_ref[r, j], 0)
        ok = (col < given) | ((col >= most) & (col - most <= step))
        t = jnp.where(ok, t, NEG)
        top = jnp.maximum(jnp.max(s, axis=1, keepdims=True), jnp.max(t, axis=1, keepdims=True))
        w = jnp.exp(s - top)
        f = jnp.exp(t - top)
        total = jnp.sum(w, axis=1, keepdims=True) + jnp.sum(f, axis=1, keepdims=True)
        got = jnp.dot(w.astype(BF16), cbuf[slot, 1], preferred_element_type=F32)
        got += jnp.dot(f.astype(BF16), values, preferred_element_type=F32)
        got = got / total
        for t_ in range(dec.shape[0]):
            for h in range(8):
                dec[t_, r:r + 1, h * 128:h * 128 + 128] = got[t_ * 8 + h:t_ * 8 + h + 1]
        if r + 2 < groups:
            cache_copy(r + 2).start()

    def place(slot):
        return (x + slot[0]) % 4, (yhi + slot[1]) % 2

    def query_unit(unit):
        slot = unit[0][1] * 4 + unit[0][0]
        xs, yhs = place(unit[0])
        start, size = row_range(unit[1], CUT_Q, chunk)
        gq.shared(*unit)

        @pl.loop(0, 8)
        def _(j):
            lane = j // 4
            cols = pl.ds(pl.multiple_of((j % 4) * 256, 256), 256)
            r = yhs * 8 + xs * 2 + c + lane * (1 - 2 * c)
            acc[:, cols] += jnp.dot(
                tok[r, :, start:start + size],
                wq[lane, slot, start:start + size, cols],
                preferred_element_type=F32,
            )

    query_unit(UNITS[0])
    query_unit(UNITS[1])
    waiting = []
    for k in range(len(EVENTS)):
        gq.event(k)
        if k == 1:
            swap_o.start()
        if k == START_O:
            own_o.wait()
            swap_o.wait_recv()
            go.start(START_1)
        if k == START_O + 1:
            go.start(START_2)
        for unit in waiting:
            query_unit(unit)
        waiting = EVENTS[k][2]
        if k >= 1:
            decode(k - 1)
    for unit in waiting:
        query_unit(unit)
    query[...] = acc[...].astype(BF16)

    def swap_mixed(b):
        rows = pl.ds(b * 256, 256)
        return pltpu.make_async_remote_copy(
            src_ref=mixed.at[ylo, rows],
            dst_ref=mixed.at[ylo, rows],
            send_sem=ms.at[b],
            recv_sem=mr.at[b],
            device_id=near["yl"],
            device_id_type=MESH,
        )

    for b in range(4):
        first = max(b - 1, 0) * 128
        rows = slice(b * 128, b * 128 + 128)
        q8 = jnp.concatenate([query[rows, h * 128:h * 128 + 128] for h in range(8)], axis=0)
        keys = kvs[first:first + 256, 0:128]
        values = kvs[first:first + 256, 128:256]
        s = lax.dot_general(q8, keys, (((1,), (1,)), ((), ())), preferred_element_type=F32) * scale
        row = lax.broadcasted_iota(jnp.int32, (128, 1), 0) + b * 128
        col = lax.broadcasted_iota(jnp.int32, (1, 256), 1) + first
        begin = jnp.zeros((128, 1), jnp.int32)
        for n, end in zip(lens, ends):
            begin += jnp.where(row >= end, n, 0)
        bias = jnp.where((col >= begin) & (col <= row), 0.0, NEG)
        s = (s.reshape(8, 128, 256) + bias[None]).reshape(1024, 256)
        w = jnp.exp(s - jnp.max(s, axis=1, keepdims=True))
        total = jnp.sum(w, axis=1, keepdims=True)
        o = jnp.dot(w.astype(BF16), values, preferred_element_type=F32) / total
        o = o.astype(BF16)
        for h in range(8):
            mixed[ylo, rows, h * 128:h * 128 + 128] = o[h * 128:h * 128 + 128]
        if b % 2 == 1:
            swap_mixed(b // 2).start()
        if b >= 1 and b < 3:
            go.event(b - 1)

    def role(slot):
        xs, yhs = place(slot)
        zs = yhs * 2 + xs // 2
        return (z + 4 - zs) % 4, zs, xs % 2

    def item(k):
        source, parts, row, rows = ITEMS[k]
        return source, source[1] * 4 + source[0], row, rows, *row_range(parts, CUT_O, half)

    def far_copy(k, which):
        source, slot, row, rows, start, size = item(k)
        return pltpu.make_async_remote_copy(
            src_ref=tok.at[pl.ds(2 * slot, 2), pl.ds(row + which * (rows // 2), rows // 2), pl.ds(start, size)],
            dst_ref=rh.at[slot, :, pl.ds(row // 2, rows // 2), pl.ds(start, size)],
            send_sem=hs2.at[k, which],
            recv_sem=hr2.at[k, which],
            device_id=near["z3" if which else "z1"],
            device_id_type=MESH,
        )

    def near_copy(k, which, part):
        source, slot, row, rows, start, size = item(k)
        at = pl.ds(row + part * (rows // 2), rows // 2)
        return pltpu.make_async_remote_copy(
            src_ref=tok.at[pl.ds(2 * slot, 2), at, pl.ds(start, size)],
            dst_ref=rf.at[role(source)[2], which, :, at, pl.ds(start, size)],
            send_sem=fs.at[k, part],
            recv_sem=fr.at[k, which * 2 + part],
            device_id=near["z3" if which else "z1"],
            device_id_type=MESH,
        )

    def out_cols(lane, start):
        return pl.multiple_of((c + lane * (1 - 2 * c)) * chunk + e * half + start, 128)

    def y_copy(k, lane):
        source, slot, row, rows, start, size = item(k)
        return pltpu.make_async_remote_copy(
            src_ref=tok.at[2 * slot + lane, pl.ds(row, rows), pl.ds(start, size)],
            dst_ref=out_ref.at[pl.ds(row, rows), pl.ds(out_cols(lane, start), size)],
            send_sem=ys.at[k, lane],
            recv_sem=yr.at[k, lane],
            device_id=near["yl"],
            device_id_type=MESH,
        )

    def part_item(k):
        source, slot, row, rows, start, size = item(k)
        if row == 0:
            go.shared(source, ITEMS[k][1])

        @pl.loop(0, 2)
        def _(lane):
            by_head = (((1,), (1,)), ((), ()))
            total = lax.dot_general(
                mixed[0, row:row + rows],
                wo[lane, slot, 0, start:start + size, :],
                by_head,
                preferred_element_type=F32,
            )
            total += lax.dot_general(
                mixed[1, row:row + rows],
                wo[lane, slot, 1, start:start + size, :],
                by_head,
                preferred_element_type=F32,
            )
            tok[2 * slot + lane, row:row + rows, start:start + size] = total.astype(BF16)

        dz, _, _ = role(source)

        @pl.when(dz == 2)
        def _():
            far_copy(k, 0).start()
            far_copy(k, 1).start()

        for which in range(2):

            @pl.when(dz == (1 if which else 3))
            def _():
                near_copy(k, which, 1 - which).start()

    STEP = 64

    def pass_on(k):
        source, slot, row, rows, start, size = item(k)
        dz, _, _ = role(source)
        for which in range(2):

            @pl.when(dz == (1 if which else 3))
            def _():
                far_copy(k, which).wait_recv()
                steps = rows // 2 // STEP

                @pl.loop(0, 2 * steps)
                def _(j):
                    lane = j // steps
                    i = pl.multiple_of((j % steps) * STEP, STEP)
                    at = pl.ds(row + which * (rows // 2) + i, STEP)
                    total = tok[2 * slot + lane, at, start:start + size].astype(F32)
                    total += rh[slot, lane, pl.ds(row // 2 + i, STEP), start:start + size].astype(F32)
                    tok[2 * slot + lane, at, start:start + size] = total.astype(BF16)

                near_copy(k, which, which).start()

    def collect(k):
        source, slot, row, rows, start, size = item(k)
        dz, _, ylos = role(source)

        @pl.when(dz == 0)
        def _():
            for which in range(2):
                for part in range(2):
                    near_copy(k, which, part).wait_recv()

            def summed(j):
                lane = j // (rows // STEP)
                at = pl.ds(pl.multiple_of(row + (j % (rows // STEP)) * STEP, STEP), STEP)
                total = tok[2 * slot + lane, at, start:start + size].astype(F32)
                for d in range(2):
                    total += rf[ylos, d, lane, at, start:start + size].astype(F32)
                return lane, at, total.astype(BF16)

            @pl.when(ylos == ylo)
            def _():
                @pl.loop(0, 2 * (rows // STEP))
                def _(j):
                    lane, at, total = summed(j)
                    out_ref[at, pl.ds(out_cols(lane, start), size)] = total

            @pl.when(ylos != ylo)
            def _():
                @pl.loop(0, 2 * (rows // STEP))
                def _(j):
                    lane, at, total = summed(j)
                    tok[2 * slot + lane, at, start:start + size] = total

                for lane in range(2):
                    y_copy(k, lane).start()

    for what, k in PLAN:
        if what == "mixed":
            swap_mixed(k).wait_recv()
        elif what == "event":
            go.event(k)
        elif what == "part":
            part_item(k)
        elif what == "pass":
            pass_on(k)
        elif what == "decode":
            decode(k)
        else:
            collect(k)

    dec_ref[...] = dec[...].astype(BF16)
    gq.finish()
    go.finish()
    swap_o.wait_send()
    for i in range(1, groups):
        handoff(i).wait_send()
    for b in range(2):
        swap_mixed(b).wait_send()
    for k in range(len(ITEMS)):
        dz, _, ylos = role(ITEMS[k][0])

        @pl.when(dz == 2)
        def _():
            far_copy(k, 0).wait_send()
            far_copy(k, 1).wait_send()

        for which in range(2):

            @pl.when(dz == (1 if which else 3))
            def _():
                near_copy(k, which, 0).wait_send()
                near_copy(k, which, 1).wait_send()

        @pl.when((dz == 0) & (ylos != ylo))
        def _():
            for lane in range(2):
                y_copy(k, lane).wait_send()

        @pl.when((dz == 0) & (ylos == ylo))
        def _():
            for lane in range(2):
                y_copy(k, lane).wait_recv()


def layer(tokens, wq, wkv, wo, cache, fresh, decode_query, cache_len, new_len, route):
    count, model = tokens.shape
    requests, most, span = (fresh.shape[0], fresh.shape[2], cache.shape[2])
    rows, cols = wq.shape
    any_ = pl.BlockSpec(memory_space=pl.ANY)
    vmem = pl.BlockSpec(memory_space=pltpu.VMEM)
    smem = pl.BlockSpec(memory_space=pltpu.SMEM)
    dma = pltpu.SemaphoreType.DMA
    out_dec = (decode_query.shape[1] // 8, requests, 8 * 128)
    n = len(ITEMS)
    return pl.pallas_call(
        layer_kernel,
        name="layer",
        out_shape=(
            jax.ShapeDtypeStruct((count, cols), BF16),
            jax.ShapeDtypeStruct(out_dec, BF16),
        ),
        in_specs=[any_, any_, any_, any_, any_, vmem, vmem, smem, smem, smem],
        out_specs=(vmem, vmem),
        scratch_shapes=[
            pltpu.VMEM((16, count, 512), BF16),
            pltpu.VMEM((2, 8, rows, cols), BF16),
            pltpu.VMEM((2, 8, 2, rows // 2, cols), BF16),
            pltpu.VMEM((count, cols), F32),
            pltpu.VMEM((count, cols), BF16),
            pltpu.VMEM((2, count, cols), BF16),
            pltpu.VMEM((8, 2, count // 2, 256), BF16),
            pltpu.VMEM((2, 2, 2, count, 256), BF16),
            pltpu.VMEM((2, 512, 256), BF16),
            pltpu.VMEM((count, 256), BF16),
            pltpu.VMEM((requests, most, 256), BF16),
            pltpu.VMEM((requests, most, 256), BF16),
            pltpu.VMEM((2, 2, span, 128), BF16),
            pltpu.VMEM(out_dec, F32),
            dma((len(MOVES_ALL),)), dma((len(MOVES_ALL),)), dma((len(MOVES_ALL),)), dma((len(MOVES_ALL),)),
            dma((2,)), dma((2,)), dma((1,)), dma((1,)),
            dma((n, 2)), dma((n, 2)), dma((n, 2)), dma((n, 4)), dma((n, 2)), dma((n, 2)),
            dma((16,)), dma((2,)), dma((2,)), dma((requests,)), dma((requests,)), dma((2,)),
        ],
        compiler_params=pltpu.CompilerParams(
            collective_id=0, has_side_effects=True, vmem_limit_bytes=63 * 2**20
        ),
    )(tokens, wq, wkv, wo, cache, fresh, decode_query, cache_len, new_len, route)


def local(
    tokens, w_query, w_keyval, output_weight, cache, fresh, decode_query, cache_len, new_len, route
):
    count, model = tokens.shape
    slots = route.shape[1]
    steps, rows, qcols = decode_query.shape
    width = w_keyval.shape[2] // 2
    heads = qcols // width
    most = 2 * count // slots
    extra = jnp.pad(jnp.transpose(fresh, (2, 0, 1, 3)), ((0, 0), (0, 0), (0, most - steps), (0, 0)))
    dq = decode_query.reshape(steps, rows, heads, width).transpose(1, 0, 2, 3).reshape(rows, steps * heads, width)
    prefill_out, decoded = layer(
        tokens,
        w_query.reshape(w_query.shape[0], -1),
        w_keyval.reshape(model, -1),
        output_weight.reshape(output_weight.shape[0], -1),
        cache,
        extra,
        dq,
        cache_len,
        new_len,
        route,
    )
    return (prefill_out, decoded)


def solution(mesh):
    placed = (
        P("req", None),
        P("req", "tp", None),
        P(None, "tp", None),
        P("req", "tp", None),
        P(None, "req", None, "tp"),
        P(None, None, "req", "tp"),
        P(None, "req", "tp"),
        P("req", None),
        P(),
        P(),
    )
    return jax.shard_map(
        local,
        mesh=mesh,
        in_specs=placed,
        out_specs=(P("req", "tp"), P(None, "req", "tp")),
        check_vma=False,
    )
```
